256 devices in a mesh: store: 32 (over y, z), tp: 8 (over x, core).
Axes of the slice: x: 4, y: 4, z: 8, core: 2. Of those that a mesh axis runs over, the one named last changes fastest.
Arguments:
- hidden: bfloat16 [16384, 8192], P('store', 'tp'), may hold values from -6 to 6
- gain: bfloat16 [8192], replicated, may hold values from 0.099609375 to 1.8984375
- w_query: bfloat16 [8192, 4096], P('store', 'tp'), may hold values from -0.09375 to 0.09375
- key_matrix: bfloat16 [8192, 1024], P('store', 'tp'), may hold values from -0.09375 to 0.09375
- value_matrix: bfloat16 [8192, 1024], P('store', 'tp'), may hold values from -0.1875 to 0.1875
- passage_cache: bfloat16 [128, 1024, 2048], P(None, 'store', 'tp'), may hold values from -330 to 330
- passage_ids: int32 [32, 6], P('store'), may hold values from 0 to 127
- placement: int32 [128], replicated, may hold values from 0 to 31
- tile_index: int32 [32, 4], P('store'), may hold values from 0 to 47, as said below
- tile_count: int32 [32], P('store'), may hold values from 1 to 4, 64 in all
Outputs:
- attended: bfloat16 [16384, 4096], P('store', 'tp')
The draws below stay inside these ranges and needn't reach their ends.
Inputs may be any that keep to these rules, and one draw needn't show every extreme that they name: `tile_index`: the tiles of one request are distinct. Slots from tile_count[r] on are unused; some request uses all 4.
All inputs are finite; a program needn't handle non-finite values. No bound on the sum of `tile_count` on one device may be relied on, other than what follows from the above.
Results may differ from the reference program's by a relative error of at most 0.025.
Values may be sent and summed in bfloat16 or wider, within the bound.
A program may use at most 128 MiB of HBM per device.

```python
import math
import jax
import jax.numpy as jnp
import numpy as np
from jax import lax

MODEL_WIDTH = 8192
QUERY_HEADS = 32
KEY_VALUE_HEADS = 8
HEAD_SIZE = 128
LISTED_PASSAGES = 6
PASSAGE_LENGTH = 1024
TILE = 128
MAX_TILES = 4
STORED_PASSAGES = 128
REQUESTS = 32
STRIPE = 32
RECOMPUTED_SLOTS = 512
QROWS = 16384
N_STORE = 32


def draw_passage_cache(key, part):
    key = jax.random.fold_in(key, 11)
    noise_key = jax.random.fold_in(key, 0)
    array_shape = (STORED_PASSAGES, PASSAGE_LENGTH, KEY_VALUE_HEADS, 2, HEAD_SIZE)
    column_scale = jnp.array([1.4, 3.0], jnp.float32).reshape(1, 1, 1, 2, 1)
    value_rows = jnp.clip(jax.random.normal(noise_key, array_shape, jnp.float32), -6.0, 6.0) * column_scale
    return value_rows.reshape(STORED_PASSAGES, PASSAGE_LENGTH, KEY_VALUE_HEADS * 2 * HEAD_SIZE).astype(jnp.bfloat16)


def draw_tile_index(key, part):
    key = jax.random.fold_in(key, 23)
    request_keys = jax.random.split(key, REQUESTS)

    def one_request(request_key):
        return jax.random.permutation(request_key, LISTED_PASSAGES * PASSAGE_LENGTH // TILE)[:MAX_TILES]
    return jax.vmap(one_request)(request_keys).astype(jnp.int32)


def touch_ends(values, key, low, top_value):
    spot = [jax.random.randint(jax.random.fold_in(key, axis), (), 0, length) for axis, length in enumerate(values.shape)]
    widest = values.shape.index(max(values.shape))
    next_to = spot[:widest] + [(spot[widest] + 1) % values.shape[widest]] + spot[widest + 1:]
    return values.at[tuple(spot)].set(low).at[tuple(next_to)].set(top_value)


def shard_levels(own_key, dims, cuts, low, largest):
    level = 1.0
    for dim, blocks in cuts:
        draws = jax.random.uniform(jax.random.fold_in(jax.random.fold_in(own_key, 6), dim), (blocks,), jnp.float32, low / len(cuts), largest / len(cuts))
        level = level * jnp.repeat(jnp.exp(draws), dims[dim] // blocks).reshape((-1,) + (1,) * (len(dims) - 1 - dim))
    return level


def rank_table(count, slope):
    portions = [(1 << 20) // math.isqrt(rank ** slope) + 1 for rank in range(1, count + 1)]
    width = 1 + sum(portions) // (1 << 30)
    return np.cumsum(np.array([max(1, weight // width) for weight in portions]))


def ranked(key, extent, count, skew):
    listing = rank_table(count, skew)
    lot = jax.random.randint(jax.random.fold_in(key, 1), extent, 0, int(listing[count - 1]))
    grade = jnp.searchsorted(jnp.asarray(listing, jnp.int32), lot, side="right")
    return jax.random.permutation(jax.random.fold_in(key, 2), count)[grade].astype(jnp.int32)


def split_up(number_of, total, limit, slope):
    loads = [(1 << 20) // math.isqrt(standing ** slope) + 1 for standing in range(2, number_of + 1)]
    rest, given = total - limit - (number_of - 1), [1] * (number_of - 1)
    while rest > 0:
        free = [i for i in range(number_of - 1) if given[i] < limit]
        mass, remaining = sum([loads[i] for i in free]), rest
        for i in free:
            addition = min(limit - given[i], max(1, remaining * loads[i] // mass), rest)
            given[i] = given[i] + addition
            rest = rest - addition
    return np.array([limit] + given)


def ragged(own_key, count, total, bound, skew):
    if count == 2:
        one = jax.random.randint(own_key, (), max(1, total - bound), min(bound, total - 1) + 1)
        return jnp.stack([one, total - one])
    sizes = jnp.asarray(split_up(count, total, bound, skew), jnp.int32)
    pairs = (count - 1) // 2
    donor, taker = sizes[1:1 + 2 * pairs:2], sizes[2:2 + 2 * pairs:2]
    slack = jnp.minimum(donor - 1, bound - taker)
    moved = jax.random.randint(jax.random.fold_in(own_key, 1), (pairs,), 0, 1 << 20) % (slack + 1)
    sizes = sizes.at[1:1 + 2 * pairs:2].set(donor - moved).at[2:2 + 2 * pairs:2].set(taker + moved)
    return sizes[jax.random.permutation(jax.random.fold_in(own_key, 2), count)]


def bell_draw(key, extent, spread, limit, pieces=(), kind=jnp.bfloat16):
    values = spread * jax.random.normal(key, extent, jnp.float32)
    if pieces:
        values = values * shard_levels(key, extent, pieces, -0.22, 0.18)
    return jnp.clip(values, -limit, limit).astype(kind)


def setup_inputs(seed: int = 0) -> dict:
    streams_of = jax.random.split(jax.random.key(seed), 11)
    hidden = bell_draw(streams_of[0], (QROWS, MODEL_WIDTH), 1.0, 6.0, ((0, 32), (1, 8)))
    gain = jnp.clip(1.0 + 0.18 * jax.random.normal(streams_of[1], (MODEL_WIDTH,), jnp.float32), 0.099609375, 1.8984375).astype(jnp.bfloat16)
    w_query = bell_draw(streams_of[2], (MODEL_WIDTH, QUERY_HEADS * HEAD_SIZE), (MODEL_WIDTH // 2) ** -0.5, 0.09375, ((0, 32), (1, 8)))
    key_matrix = bell_draw(streams_of[3], (MODEL_WIDTH, KEY_VALUE_HEADS * HEAD_SIZE), (MODEL_WIDTH // 2) ** -0.5, 0.09375, ((0, 32), (1, 8)))
    value_matrix = bell_draw(streams_of[4], (MODEL_WIDTH, KEY_VALUE_HEADS * HEAD_SIZE), (MODEL_WIDTH // 8) ** -0.5, 0.1875, ((0, 32), (1, 8)))
    passage_cache = draw_passage_cache(jax.random.fold_in(streams_of[10], 71), 0)
    passage_ids = touch_ends(ranked(streams_of[6], (REQUESTS, LISTED_PASSAGES), STORED_PASSAGES, 2), jax.random.fold_in(streams_of[6], 3), 0, STORED_PASSAGES - 1).astype(jnp.int32)
    placement = touch_ends(jax.random.randint(streams_of[7], (STORED_PASSAGES,), 0, N_STORE), jax.random.fold_in(streams_of[7], 1), 0, N_STORE - 1).astype(jnp.int32)
    tile_index = draw_tile_index(jax.random.fold_in(streams_of[10], 71), 0)
    tile_count = ragged(streams_of[9], REQUESTS, MAX_TILES * REQUESTS // 2, MAX_TILES, 2).astype(jnp.int32)
    return {"hidden": hidden, "gain": gain, "w_query": w_query, "key_matrix": key_matrix, "value_matrix": value_matrix, "passage_cache": passage_cache, "passage_ids": passage_ids, "placement": placement, "tile_index": tile_index, "tile_count": tile_count}


def rotate_pairs(vectors, positions):
    half_size = vectors.shape[-1] // 2
    exponent = jnp.arange(half_size, dtype=jnp.float32) * (2.0 / vectors.shape[-1])
    frequency = jnp.exp(-math.log(500000.0) * exponent)
    angles = positions.astype(jnp.float32)[:, None] * frequency[None, :]
    cosine = jnp.cos(angles)[:, None, :]
    sine = jnp.sin(angles)[:, None, :]
    first_half = vectors[..., :half_size]
    second_half = vectors[..., half_size:]
    return jnp.concatenate([first_half * cosine - second_half * sine, second_half * cosine + first_half * sine], axis=-1)

def attend_heads(query_rot, keys, value_rows, allowed, query_group_size):
    score_scale = 1.0 / math.sqrt(query_rot.shape[-1])

    def one_head(head_index):
        query_head = lax.dynamic_index_in_dim(query_rot, head_index, 1, keepdims=False)
        kv_index = head_index // query_group_size
        key_head = lax.dynamic_index_in_dim(keys, kv_index, 1, keepdims=False)
        value_head = lax.dynamic_index_in_dim(value_rows, kv_index, 1, keepdims=False)
        scores = lax.dot_general(query_head, key_head, (((1,), (1,)), ((), ())), preferred_element_type=jnp.float32) * score_scale
        scores = jnp.where(allowed, scores, -jnp.inf)
        highest = lax.optimization_barrier(jnp.max(scores, axis=1, keepdims=True))
        exponent_terms = jnp.exp(scores - highest)
        weights = (exponent_terms / lax.optimization_barrier(jnp.sum(exponent_terms, axis=1, keepdims=True))).astype(jnp.bfloat16)
        return jnp.dot(weights, value_head, preferred_element_type=jnp.float32)
    return lax.map(one_head, jnp.arange(query_rot.shape[1], dtype=jnp.int32))

def reference(hidden, gain, w_query, key_matrix, value_matrix, passage_cache, passage_ids, placement, tile_index, tile_count):
    query_group_size = QUERY_HEADS // KEY_VALUE_HEADS

    def one_request(bundle):
        token_rows, request_passage_index, request_tiles, request_count = bundle
        raw_values = token_rows.astype(jnp.float32)
        inverse_rms = lax.rsqrt(lax.optimization_barrier(jnp.mean(raw_values * raw_values, axis=1, keepdims=True)) + 1e-05)
        normed_input = (raw_values * inverse_rms * gain.astype(jnp.float32)).astype(jnp.bfloat16)
        query = jnp.dot(normed_input, w_query, preferred_element_type=jnp.float32).reshape(RECOMPUTED_SLOTS, QUERY_HEADS, HEAD_SIZE)
        recomputed_key = jnp.dot(normed_input, key_matrix, preferred_element_type=jnp.float32).reshape(RECOMPUTED_SLOTS, KEY_VALUE_HEADS, HEAD_SIZE)
        recomputed_value = jnp.dot(normed_input, value_matrix, preferred_element_type=jnp.float32).reshape(RECOMPUTED_SLOTS, KEY_VALUE_HEADS, HEAD_SIZE)
        positions = (request_tiles[:, None] * TILE + jnp.arange(TILE, dtype=jnp.int32)[None, :]).reshape(RECOMPUTED_SLOTS)
        query_rot = rotate_pairs(query, positions).astype(jnp.bfloat16)
        rotated_key = rotate_pairs(recomputed_key, positions).astype(jnp.bfloat16)
        fresh_rows = jnp.stack([rotated_key, recomputed_value.astype(jnp.bfloat16)], axis=2).reshape(RECOMPUTED_SLOTS, KEY_VALUE_HEADS * 2 * HEAD_SIZE)

        def single_passage(passage):
            block = lax.dynamic_index_in_dim(passage_cache, passage, 0, keepdims=False)
            order = (jnp.arange(PASSAGE_LENGTH, dtype=jnp.int32) - placement[passage] * STRIPE) % PASSAGE_LENGTH
            return block[order]
        context_output = jax.vmap(single_passage)(request_passage_index).reshape(LISTED_PASSAGES * PASSAGE_LENGTH, KEY_VALUE_HEADS * 2 * HEAD_SIZE)
        for tile_slot in range(MAX_TILES):
            start = (request_tiles[tile_slot] * TILE).astype(jnp.int32)
            current = lax.dynamic_slice_in_dim(context_output, start, TILE, 0)
            update = jnp.where(tile_slot < request_count, fresh_rows[tile_slot * TILE:(tile_slot + 1) * TILE], current)
            context_output = lax.dynamic_update_slice_in_dim(context_output, update, start, 0)
        blended_cache = context_output.reshape(LISTED_PASSAGES * PASSAGE_LENGTH, KEY_VALUE_HEADS, 2, HEAD_SIZE)
        allowed = jnp.arange(LISTED_PASSAGES * PASSAGE_LENGTH, dtype=jnp.int32)[None, :] <= positions[:, None]
        heads_out = attend_heads(query_rot, blended_cache[:, :, 0, :], blended_cache[:, :, 1, :], allowed, query_group_size)
        valid = jnp.arange(RECOMPUTED_SLOTS, dtype=jnp.int32) // TILE < request_count
        result = jnp.where(valid[:, None, None], jnp.transpose(heads_out, (1, 0, 2)), jnp.float32(0.0))
        return result.reshape(RECOMPUTED_SLOTS, QUERY_HEADS * HEAD_SIZE).astype(jnp.bfloat16)
    stacked = lax.map(one_request, (hidden.reshape(REQUESTS, RECOMPUTED_SLOTS, MODEL_WIDTH), passage_ids, tile_index, tile_count))
    return stacked.reshape(REQUESTS * RECOMPUTED_SLOTS, QUERY_HEADS * HEAD_SIZE)
```

```python
import math

import jax
import jax.numpy as jnp
from jax import lax
from jax.experimental import pallas as pl
from jax.experimental.pallas import tpu as pltpu
from jax.sharding import PartitionSpec as P

HEAD = 128
NY, NZ, NX = 4, 8, 4
N_STORE = NY * NZ
N_TP = 2 * NX
SLOTS = 512
TILE = 128
PASSAGES = 6
STRIPE = 32
CHUNK = 256
COLS = 768
FEATS = 1024
KEEP = 192
FULL = (0, CHUNK)
ZFIRST = (0, KEEP)
YFIRST = (KEEP, CHUNK)
MESH_ID = pl.DeviceIdType.MESH
SCORE = math.log2(math.e) / math.sqrt(HEAD)


def halves(rows):
    low, high = rows
    middle = (low + high) // 2
    return (low, middle), (middle, high)


def exchange_kernel(
    hidden, gain, wq, km, vm, cache, ids, tiles,
    q_out, kv_out, inbox,
    hbuf, wbuf, cbuf, outbox, idrow, idbuf, idmem, acc,
    load_sem, zr, zl, yu, yd, yu2, yd2, br, bl, hx, hs, idr, pr,
    zs, ys, ys2, bs, hxs, hss, ids_s, ps,
):
    st = lax.axis_index("store")
    tp = lax.axis_index("tp")
    y, z = st // NZ, st % NZ
    x, core = tp // 2, tp % 2
    sibling = x * 2 + (1 - core)

    def at_z(k):
        return y * NZ + (z + k + NZ) % NZ

    def at_y(k):
        return ((y + k + NY) % NY) * NZ + z

    def slot(dy, dz):
        return ((y + dy + NY) % NY) * NZ + (z + dz + NZ) % NZ

    def at_x(k):
        return ((x + k + NX) % NX) * 2 + core

    loads = [
        pltpu.make_async_copy(wq, wbuf.at[st, :, pl.ds(0, 512)], load_sem.at[0]),
        pltpu.make_async_copy(km, wbuf.at[st, :, pl.ds(512, 128)], load_sem.at[1]),
        pltpu.make_async_copy(vm, wbuf.at[st, :, pl.ds(640, 128)], load_sem.at[2]),
        pltpu.make_async_copy(hidden, hbuf.at[tp], load_sem.at[3]),
        pltpu.make_async_copy(cache, cbuf, load_sem.at[4]),
    ]
    for load in loads:
        load.start()
    idrow[...] = jnp.zeros_like(idrow)
    idrow[0:1, 0:PASSAGES] = ids[...]

    barrier = pltpu.get_barrier_semaphore()

    def greet(d, carry):
        pl.semaphore_signal(
            barrier, inc=1, device_id=((st + d) % N_STORE, tp), device_id_type=MESH_ID
        )
        return carry

    lax.fori_loop(1, N_STORE, greet, 0)
    for peer in (at_x(1), at_x(-1), sibling):
        pl.semaphore_signal(barrier, inc=1, device_id=(st, peer), device_id_type=MESH_ID)
    pl.semaphore_wait(barrier, N_STORE - 1 + 3)

    pending = []

    def send(ref, send_sem, recv_sem, store, peer, later=True):
        copy = pltpu.make_async_remote_copy(
            src_ref=ref, dst_ref=ref, send_sem=send_sem, recv_sem=recv_sem,
            device_id=(store, peer), device_id_type=MESH_ID,
        )
        copy.start()
        if later:
            pending.append(copy)
        return copy

    def arrived(ref, sem):
        pltpu.make_async_copy(ref, ref, sem).wait()

    def w_at(chunk, rows):
        return wbuf.at[chunk, pl.ds(rows[0], rows[1] - rows[0]), :]

    def id_copy(d):
        other = (st + d) % N_STORE
        return pltpu.make_async_remote_copy(
            src_ref=idrow, dst_ref=idbuf.at[st], send_sem=ids_s.at[d], recv_sem=idr.at[d],
            device_id=(other, tp), device_id_type=MESH_ID,
        )

    def id_start(d, carry):
        id_copy(d).start()
        return carry

    lax.fori_loop(1, N_STORE, id_start, 0)

    for load in loads:
        load.wait()
    own = w_at(st, FULL)
    send(own, zs.at[0], zr.at[1], at_z(1), tp)
    send(own, zs.at[1], zl.at[1], at_z(-1), tp)
    send(own, ys.at[0], yu.at[0], at_y(1), tp)
    send(own, ys.at[1], yd.at[0], at_y(-1), tp)
    h_sends = []
    h_own = hbuf.at[tp]
    h_sends.append(send(h_own, hxs.at[0], hx.at[0], st, at_x(1), False))
    h_sends.append(send(h_own, hxs.at[1], hx.at[1], st, at_x(-1), False))
    h_sends.append(send(h_own, hss.at[0], hs.at[0], st, sibling, False))

    idbuf[pl.ds(st, 1), :, :] = idrow[...].reshape(1, 1, 128)

    def id_wait(d, carry):
        other = (st - d + N_STORE) % N_STORE
        arrived(idbuf.at[other], idr.at[d])
        return carry

    lax.fori_loop(1, N_STORE, id_wait, 0)
    to_scalar = pltpu.make_async_copy(idbuf, idmem, load_sem.at[0])
    to_scalar.start()
    to_scalar.wait()

    def stripe_copy(d):
        other = (st + d) % N_STORE
        return pltpu.make_async_remote_copy(
            src_ref=outbox.at[other], dst_ref=inbox.at[st], send_sem=ps.at[d], recv_sem=pr.at[d],
            device_id=(other, tp), device_id_type=MESH_ID,
        )

    def fill(other):
        for j in range(PASSAGES):
            outbox[other, j * STRIPE : (j + 1) * STRIPE, :] = cbuf[idmem[other, 0, j]]

    def stripe_start(d, carry):
        fill((st + d) % N_STORE)
        stripe_copy(d).start()
        return carry

    lax.fori_loop(1, N_STORE, stripe_start, 0)
    fill(st)
    own_stripes = pltpu.make_async_copy(outbox.at[st], inbox.at[st], load_sem.at[1])
    own_stripes.start()

    def project(chunk):
        piece = chunk // 4
        column = pl.multiple_of((chunk % 4) * CHUNK, CHUNK)
        for m in range(2):
            rows = slice(m * 256, (m + 1) * 256)
            acc[rows, :] += jnp.dot(
                hbuf[piece, rows, pl.ds(column, CHUNK)], wbuf[chunk], preferred_element_type=jnp.float32
            )

    offsets = [0, -1, 1, -2, 2, -3, 3, 4]

    def forward_y(i):
        ref = w_at(slot(0, offsets[i]), ZFIRST)
        send(ref, ys.at[2 * i], yu.at[i], at_y(1), tp)
        send(ref, ys.at[2 * i + 1], yd.at[i], at_y(-1), tp)

    def ring(k):
        if k < 4:
            low, high = slot(0, -k), slot(0, k)
            arrived(w_at(low, FULL), zr.at[k])
            part = FULL if k < 3 else halves(FULL)[0]
            send(w_at(low, part), zs.at[2 * k], zr.at[k + 1], at_z(1), tp)
            arrived(w_at(high, FULL), zl.at[k])
            part = FULL if k < 3 else halves(FULL)[1]
            send(w_at(high, part), zs.at[2 * k + 1], zl.at[k + 1], at_z(-1), tp)
            forward_y(2 * k - 1)
            forward_y(2 * k)
        else:
            far = slot(0, 4)
            arrived(w_at(far, halves(FULL)[0]), zr.at[4])
            arrived(w_at(far, halves(FULL)[1]), zl.at[4])
            forward_y(7)

    def y_near(i):
        rows = FULL if i == 0 else ZFIRST
        top, bottom = halves(rows)
        below, above = slot(-1, offsets[i]), slot(1, offsets[i])
        arrived(w_at(below, rows), yu.at[i])
        send(w_at(below, top), ys2.at[2 * i], yu2.at[i], at_y(1), tp)
        arrived(w_at(above, rows), yd.at[i])
        send(w_at(above, bottom), ys2.at[2 * i + 1], yd2.at[i], at_y(-1), tp)

    def y_far(i):
        rows = FULL if i == 0 else ZFIRST
        top, bottom = halves(rows)
        far = slot(2, offsets[i])
        arrived(w_at(far, top), yu2.at[i])
        arrived(w_at(far, bottom), yd2.at[i])

    lines = [-1, 1, 2]

    def line_start(j):
        ref = w_at(slot(lines[j], 0), YFIRST)
        send(ref, bs.at[j, 0], br.at[j, 1], at_z(1), tp)
        send(ref, bs.at[j, 1], bl.at[j, 1], at_z(-1), tp)

    def line(j, k):
        if k < 4:
            low, high = slot(lines[j], -k), slot(lines[j], k)
            arrived(w_at(low, YFIRST), br.at[j, k])
            part = YFIRST if k < 3 else halves(YFIRST)[0]
            send(w_at(low, part), bs.at[j, 2 * k], br.at[j, k + 1], at_z(1), tp)
            arrived(w_at(high, YFIRST), bl.at[j, k])
            part = YFIRST if k < 3 else halves(YFIRST)[1]
            send(w_at(high, part), bs.at[j, 2 * k + 1], bl.at[j, k + 1], at_z(-1), tp)
        else:
            far = slot(lines[j], 4)
            arrived(w_at(far, halves(YFIRST)[0]), br.at[j, 4])
            arrived(w_at(far, halves(YFIRST)[1]), bl.at[j, 4])

    def h_near():
        low, high = at_x(-1), at_x(1)
        arrived(hbuf.at[low], hx.at[0])
        h_sends.append(send(hbuf.at[low, pl.ds(0, 256), :], hxs.at[2], hx.at[2], st, at_x(1), False))
        h_sends.append(send(hbuf.at[low], hss.at[1], hs.at[1], st, sibling, False))
        arrived(hbuf.at[high], hx.at[1])
        h_sends.append(send(hbuf.at[high, pl.ds(256, 256), :], hxs.at[3], hx.at[3], st, at_x(-1), False))
        h_sends.append(send(hbuf.at[high], hss.at[2], hs.at[2], st, sibling, False))

    def h_far():
        far = at_x(2)
        arrived(hbuf.at[far, pl.ds(0, 256), :], hx.at[2])
        arrived(hbuf.at[far, pl.ds(256, 256), :], hx.at[3])
        h_sends.append(send(hbuf.at[far], hss.at[3], hs.at[3], st, sibling, False))

    def h_norm():
        for i, k in enumerate((0, -1, 1, 2)):
            piece = ((x + k + NX) % NX) * 2 + (1 - core)
            arrived(hbuf.at[piece], hs.at[i])
        for copy in h_sends:
            copy.wait_send()

        def block(b, carry):
            rows = pl.ds(pl.multiple_of(b * 32, 32), 32)
            total = jnp.zeros((32, 1), jnp.float32)
            for p in range(N_TP):
                raw = hbuf[p, rows, :].astype(jnp.float32)
                total += jnp.sum(raw * raw, axis=1, keepdims=True)
            scale = lax.rsqrt(total / (N_TP * FEATS) + 1e-05)
            for p in range(N_TP):
                raw = hbuf[p, rows, :].astype(jnp.float32)
                row_gain = gain[:, p * FEATS : (p + 1) * FEATS].astype(jnp.float32)
                hbuf[p, rows, :] = (raw * scale * row_gain).astype(jnp.bfloat16)
            return carry

        lax.fori_loop(0, SLOTS // 32, block, 0)

    acc[...] = jnp.zeros_like(acc)

    ring(1)
    y_near(0)
    line_start(0)
    line_start(1)
    ring(2)
    h_near()
    y_far(0)
    line_start(2)
    y_near(1)
    y_near(2)
    line(0, 1)
    line(1, 1)
    ring(3)
    h_far()
    y_near(3)
    y_near(4)
    line(2, 1)
    line(0, 2)
    line(1, 2)
    ring(4)
    h_norm()

    def project_row(dy):
        def step(i, carry):
            project(((y + dy + NY) % NY) * NZ + i)
            return carry

        lax.fori_loop(0, NZ, step, 0)

    y_near(5)
    y_near(6)
    line(2, 2)
    line(0, 3)
    line(1, 3)
    y_near(7)
    line(2, 3)
    project_row(0)
    line(0, 4)
    line(1, 4)
    project_row(-1)
    project_row(1)
    line(2, 4)
    for i in range(1, 8):
        y_far(i)
    project_row(2)

    lane = lax.broadcasted_iota(jnp.int32, (TILE, HEAD), 1)
    frequency = jnp.exp((lane % (HEAD // 2)).astype(jnp.float32) * (-math.log(500000.0) * 2.0 / HEAD))
    for s in range(SLOTS // TILE):
        rows = slice(s * TILE, (s + 1) * TILE)
        position = lax.broadcasted_iota(jnp.int32, (TILE, HEAD), 0) + tiles[0, s] * TILE
        angle = position.astype(jnp.float32) * frequency
        cosine = jnp.cos(angle)
        sine = jnp.where(lane < HEAD // 2, -jnp.sin(angle), jnp.sin(angle))
        for h in range(5):
            vec = acc[rows, h * HEAD : (h + 1) * HEAD]
            turned = vec * cosine + pltpu.roll(vec, HEAD // 2, 1) * sine
            if h < 4:
                q_out[h, rows, :] = turned.astype(jnp.bfloat16)
            else:
                kv_out[rows, 0:HEAD] = turned.astype(jnp.bfloat16)
        kv_out[rows, HEAD : 2 * HEAD] = acc[rows, 5 * HEAD : 6 * HEAD].astype(jnp.bfloat16)

    def stripe_wait(d, carry):
        other = (st - d + N_STORE) % N_STORE
        arrived(inbox.at[other], pr.at[d])
        stripe_copy(d).wait_send()
        id_copy(d).wait_send()
        return carry

    lax.fori_loop(1, N_STORE, stripe_wait, 0)
    own_stripes.wait()
    for copy in pending:
        copy.wait_send()


def exchange(hidden, gain, wq, km, vm, cache, ids, tiles):
    any_space = pl.BlockSpec(memory_space=pl.ANY)
    vmem = pl.BlockSpec(memory_space=pltpu.VMEM)
    smem = pl.BlockSpec(memory_space=pltpu.SMEM)
    dma = pltpu.SemaphoreType.DMA
    return pl.pallas_call(
        exchange_kernel,
        out_shape=[
            jax.ShapeDtypeStruct((4, SLOTS, HEAD), jnp.bfloat16),
            jax.ShapeDtypeStruct((SLOTS, 2 * HEAD), jnp.bfloat16),
            jax.ShapeDtypeStruct((N_STORE, PASSAGES * STRIPE, 2 * HEAD), jnp.bfloat16),
        ],
        in_specs=[any_space, vmem, any_space, any_space, any_space, any_space, vmem, smem],
        out_specs=[vmem, vmem, any_space],
        scratch_shapes=[
            pltpu.VMEM((N_TP, SLOTS, FEATS), jnp.bfloat16),
            pltpu.VMEM((N_STORE, CHUNK, COLS), jnp.bfloat16),
            pltpu.VMEM((128, STRIPE, 2 * HEAD), jnp.bfloat16),
            pltpu.VMEM((N_STORE, PASSAGES * STRIPE, 2 * HEAD), jnp.bfloat16),
            pltpu.VMEM((1, 128), jnp.int32),
            pltpu.VMEM((N_STORE, 1, 128), jnp.int32),
            pltpu.SMEM((N_STORE, 1, 128), jnp.int32),
            pltpu.VMEM((SLOTS, COLS), jnp.float32),
            dma((5,)),
            dma((5,)), dma((5,)), dma((8,)), dma((8,)), dma((8,)), dma((8,)),
            dma((3, 5)), dma((3, 5)), dma((4,)), dma((4,)), dma((32,)), dma((32,)),
            dma((8,)), dma((16,)), dma((16,)), dma((3, 8)), dma((4,)), dma((4,)), dma((32,)), dma((32,)),
        ],
        compiler_params=pltpu.CompilerParams(
            collective_id=0, has_side_effects=True, vmem_limit_bytes=48 * 2**20
        ),
    )(hidden, gain, wq, km, vm, cache, ids, tiles)


KEYS = 512


def attend_kernel(ids, placement, tiles, count, q, kv, inbox, out, context, scores, highest, total, values):
    for j in range(PASSAGES):
        turn = placement[ids[0, j]]

        def order(i, carry):
            source = (i - turn + N_STORE) % N_STORE
            rows = pl.ds(pl.multiple_of(j * 1024 + i * STRIPE, STRIPE), STRIPE)
            context[rows, :] = inbox[source, j * STRIPE : (j + 1) * STRIPE, :]
            return carry

        lax.fori_loop(0, N_STORE, order, 0)
    for s in range(SLOTS // TILE):
        @pl.when(s < count[0])
        def _():
            rows = pl.ds(pl.multiple_of(tiles[0, s] * TILE, TILE), TILE)
            context[rows, :] = kv[s * TILE : (s + 1) * TILE, :]

    def one_slot(s, carry):
        slot_rows = pl.ds(pl.multiple_of(s * TILE, TILE), TILE)

        @pl.when(s >= count[0])
        def _():
            out[slot_rows, :] = jnp.zeros((TILE, 4 * HEAD), jnp.bfloat16)

        @pl.when(s < count[0])
        def _():
            tile = tiles[0, s]
            last = tile // (KEYS // TILE)
            query = q[:, slot_rows, :].reshape(4 * TILE, HEAD)

            def block_scores(b):
                keys = context[pl.ds(pl.multiple_of(b * KEYS, KEYS), KEYS), 0:HEAD]
                return lax.dot_general(
                    query, keys, (((1,), (1,)), ((), ())), preferred_element_type=jnp.float32
                )

            def widest(block):
                top = block[:, 0:HEAD]
                for n in range(1, KEYS // HEAD):
                    top = jnp.maximum(top, block[:, n * HEAD : (n + 1) * HEAD])
                return top

            block = block_scores(last)
            row = lax.broadcasted_iota(jnp.int32, (4 * TILE, KEYS), 0) % TILE + tile * TILE
            column = lax.broadcasted_iota(jnp.int32, (4 * TILE, KEYS), 1) + last * KEYS
            block = jnp.where(column <= row, block, -jnp.inf)
            scores[last] = block
            highest[...] = widest(block)

            def first_pass(b, carry):
                block = block_scores(b)
                scores[b] = block
                highest[...] = jnp.maximum(highest[...], widest(block))
                return carry

            lax.fori_loop(0, last, first_pass, 0)
            shift = jnp.max(highest[...], axis=1, keepdims=True) * SCORE
            total[...] = jnp.zeros_like(total)
            values[...] = jnp.zeros_like(values)

            def second_pass(b, carry):
                terms = jnp.exp2(scores[b] * SCORE - shift)
                part = terms[:, 0:HEAD]
                for n in range(1, KEYS // HEAD):
                    part = part + terms[:, n * HEAD : (n + 1) * HEAD]
                total[...] += part
                rows = pl.ds(pl.multiple_of(b * KEYS, KEYS), KEYS)
                values[...] += jnp.dot(
                    terms.astype(jnp.bfloat16), context[rows, HEAD : 2 * HEAD],
                    preferred_element_type=jnp.float32,
                )
                return carry

            lax.fori_loop(0, last + 1, second_pass, 0)
            result = values[...] / jnp.sum(total[...], axis=1, keepdims=True)
            for h in range(4):
                out[slot_rows, h * HEAD : (h + 1) * HEAD] = result[h * TILE : (h + 1) * TILE, :].astype(
                    jnp.bfloat16
                )

        return carry

    lax.fori_loop(0, SLOTS // TILE, one_slot, 0)


def attend(ids, placement, tiles, count, q, kv, inbox):
    vmem = pl.BlockSpec(memory_space=pltpu.VMEM)
    smem = pl.BlockSpec(memory_space=pltpu.SMEM)
    return pl.pallas_call(
        attend_kernel,
        out_shape=jax.ShapeDtypeStruct((SLOTS, 4 * HEAD), jnp.bfloat16),
        in_specs=[smem, smem, smem, smem, vmem, vmem, vmem],
        out_specs=vmem,
        scratch_shapes=[
            pltpu.VMEM((PASSAGES * 1024, 2 * HEAD), jnp.bfloat16),
            pltpu.VMEM((PASSAGES * 1024 // KEYS, 4 * TILE, KEYS), jnp.float32),
            pltpu.VMEM((4 * TILE, HEAD), jnp.float32),
            pltpu.VMEM((4 * TILE, HEAD), jnp.float32),
            pltpu.VMEM((4 * TILE, HEAD), jnp.float32),
        ],
        compiler_params=pltpu.CompilerParams(vmem_limit_bytes=48 * 2**20),
    )(ids, placement, tiles, count, q, kv, inbox)


def local(hidden, gain, w_query, key_matrix, value_matrix, passage_cache, passage_ids, placement, tile_index, tile_count):
    q, kv, inbox = exchange(
        hidden, gain.reshape(1, -1), w_query, key_matrix, value_matrix, passage_cache, passage_ids, tile_index
    )
    return attend(passage_ids, placement, tile_index, tile_count, q, kv, inbox)


def solution(mesh):
    placed = (
        P("store", "tp"), P(), P("store", "tp"), P("store", "tp"), P("store", "tp"),
        P(None, "store", "tp"), P("store", None), P(), P("store", None), P("store"),
    )
    return jax.shard_map(local, mesh=mesh, in_specs=placed, out_specs=P("store", "tp"), check_vma=False)
```

```python
import math

import jax
import jax.numpy as jnp
from jax import lax
from jax.experimental import pallas as pl
from jax.experimental.pallas import tpu as pltpu
from jax.sharding import PartitionSpec as P

HEAD = 128
NY, NZ, NX = 4, 8, 4
N_STORE = NY * NZ
N_TP = 2 * NX
SLOTS = 512
TILE = 128
PASSAGES = 6
STRIPE = 32
CHUNK = 256
COLS = 768
FEATS = 1024
KEEP = 192
FULL = (0, CHUNK)
ZFIRST = (0, KEEP)
YFIRST = (KEEP, CHUNK)
MESH_ID = pl.DeviceIdType.MESH
SCORE = math.log2(math.e) / math.sqrt(HEAD)


def halves(rows):
    low, high = rows
    middle = (low + high) // 2
    return (low, middle), (middle, high)


def exchange_kernel(
    hidden, gain, wq, km, vm, cache, ids, tiles,
    q_out, kv_out, inbox,
    hbuf, wbuf, cbuf, outbox, idrow, idbuf, idmem, acc,
    load_sem, zr, zl, yu, yd, yu2, yd2, br, bl, hx, hs, idr, pr,
    zs, ys, ys2, bs, hxs, hss, ids_s, ps,
):
    st = lax.axis_index("store")
    tp = lax.axis_index("tp")
    y, z = st // NZ, st % NZ
    x, core = tp // 2, tp % 2
    sibling = x * 2 + (1 - core)

    def at_z(k):
        return y * NZ + (z + k + NZ) % NZ

    def at_y(k):
        return ((y + k + NY) % NY) * NZ + z

    def slot(dy, dz):
        return ((y + dy + NY) % NY) * NZ + (z + dz + NZ) % NZ

    def at_x(k):
        return ((x + k + NX) % NX) * 2 + core

    loads = [
        pltpu.make_async_copy(wq, wbuf.at[st, :, pl.ds(0, 512)], load_sem.at[0]),
        pltpu.make_async_copy(km, wbuf.at[st, :, pl.ds(512, 128)], load_sem.at[1]),
        pltpu.make_async_copy(vm, wbuf.at[st, :, pl.ds(640, 128)], load_sem.at[2]),
        pltpu.make_async_copy(hidden, hbuf.at[tp], load_sem.at[3]),
        pltpu.make_async_copy(cache, cbuf, load_sem.at[4]),
    ]
    for load in loads:
        load.start()
    idrow[...] = jnp.zeros_like(idrow)
    idrow[0:1, 0:PASSAGES] = ids[...]

    barrier = pltpu.get_barrier_semaphore()

    def greet(d, carry):
        pl.semaphore_signal(
            barrier, inc=1, device_id=((st + d) % N_STORE, tp), device_id_type=MESH_ID
        )
        return carry

    lax.fori_loop(1, N_STORE, greet, 0)
    for peer in (at_x(1), at_x(-1), sibling):
        pl.semaphore_signal(barrier, inc=1, device_id=(st, peer), device_id_type=MESH_ID)
    pl.semaphore_wait(barrier, N_STORE - 1 + 3)

    pending = []

    def send(ref, send_sem, recv_sem, store, peer, later=True):
        copy = pltpu.make_async_remote_copy(
            src_ref=ref, dst_ref=ref, send_sem=send_sem, recv_sem=recv_sem,
            device_id=(store, peer), device_id_type=MESH_ID,
        )
        copy.start()
        if later:
            pending.append(copy)
        return copy

    def arrived(ref, sem):
        pltpu.make_async_copy(ref, ref, sem).wait()

    def w_at(chunk, rows):
        return wbuf.at[chunk, pl.ds(rows[0], rows[1] - rows[0]), :]

    def id_copy(d):
        other = (st + d) % N_STORE
        return pltpu.make_async_remote_copy(
            src_ref=idrow, dst_ref=idbuf.at[st], send_sem=ids_s.at[d], recv_sem=idr.at[d],
            device_id=(other, tp), device_id_type=MESH_ID,
        )

    def id_start(d, carry):
        id_copy(d).start()
        return carry

    lax.fori_loop(1, N_STORE, id_start, 0)

    for load in loads:
        load.wait()
    own = w_at(st, FULL)
    send(own, zs.at[0], zr.at[1], at_z(1), tp)
    send(own, zs.at[1], zl.at[1], at_z(-1), tp)
    send(own, ys.at[0], yu.at[0], at_y(1), tp)
    send(own, ys.at[1], yd.at[0], at_y(-1), tp)
    h_sends = []
    h_own = hbuf.at[tp]
    h_sends.append(send(h_own, hxs.at[0], hx.at[0], st, at_x(1), False))
    h_sends.append(send(h_own, hxs.at[1], hx.at[1], st, at_x(-1), False))
    h_sends.append(send(h_own, hss.at[0], hs.at[0], st, sibling, False))

    idbuf[pl.ds(st, 1), :, :] = idrow[...].reshape(1, 1, 128)

    def id_wait(d, carry):
        other = (st - d + N_STORE) % N_STORE
        arrived(idbuf.at[other], idr.at[d])
        return carry

    lax.fori_loop(1, N_STORE, id_wait, 0)
    to_scalar = pltpu.make_async_copy(idbuf, idmem, load_sem.at[0])
    to_scalar.start()
    to_scalar.wait()

    def stripe_copy(d):
        other = (st + d) % N_STORE
        return pltpu.make_async_remote_copy(
            src_ref=outbox.at[other], dst_ref=inbox.at[st], send_sem=ps.at[d], recv_sem=pr.at[d],
            device_id=(other, tp), device_id_type=MESH_ID,
        )

    def fill(other):
        for j in range(PASSAGES):
            outbox[other, j * STRIPE : (j + 1) * STRIPE, :] = cbuf[idmem[other, 0, j]]

    def stripe_start(d, carry):
        fill((st + d) % N_STORE)
        stripe_copy(d).start()
        return carry

    fill(st)
    own_stripes = pltpu.make_async_copy(outbox.at[st], inbox.at[st], load_sem.at[1])
    own_stripes.start()

    progress = [0, 1]

    def trickle():
        progress[0] += 1
        if progress[0] > 4:
            stop = min(N_STORE, progress[1] + 2)
            for d in range(progress[1], stop):
                stripe_start(d, 0)
            progress[1] = stop

    def project(chunk):
        piece = chunk // 4
        column = pl.multiple_of((chunk % 4) * CHUNK, CHUNK)
        for m in range(2):
            rows = slice(m * 256, (m + 1) * 256)
            acc[rows, :] += jnp.dot(
                hbuf[piece, rows, pl.ds(column, CHUNK)], wbuf[chunk], preferred_element_type=jnp.float32
            )

    offsets = [0, -1, 1, -2, 2, -3, 3, 4]

    def forward_y(i):
        ref = w_at(slot(0, offsets[i]), ZFIRST)
        send(ref, ys.at[2 * i], yu.at[i], at_y(1), tp)
        send(ref, ys.at[2 * i + 1], yd.at[i], at_y(-1), tp)

    def ring(k):
        if k < 4:
            low, high = slot(0, -k), slot(0, k)
            arrived(w_at(low, FULL), zr.at[k])
            part = FULL if k < 3 else halves(FULL)[0]
            send(w_at(low, part), zs.at[2 * k], zr.at[k + 1], at_z(1), tp)
            arrived(w_at(high, FULL), zl.at[k])
            part = FULL if k < 3 else halves(FULL)[1]
            send(w_at(high, part), zs.at[2 * k + 1], zl.at[k + 1], at_z(-1), tp)
            forward_y(2 * k - 1)
            forward_y(2 * k)
        else:
            far = slot(0, 4)
            arrived(w_at(far, halves(FULL)[0]), zr.at[4])
            arrived(w_at(far, halves(FULL)[1]), zl.at[4])
            forward_y(7)

    def y_near(i):
        rows = FULL if i == 0 else ZFIRST
        top, bottom = halves(rows)
        below, above = slot(-1, offsets[i]), slot(1, offsets[i])
        arrived(w_at(below, rows), yu.at[i])
        send(w_at(below, top), ys2.at[2 * i], yu2.at[i], at_y(1), tp)
        arrived(w_at(above, rows), yd.at[i])
        send(w_at(above, bottom), ys2.at[2 * i + 1], yd2.at[i], at_y(-1), tp)

    def y_far(i):
        rows = FULL if i == 0 else ZFIRST
        top, bottom = halves(rows)
        far = slot(2, offsets[i])
        arrived(w_at(far, top), yu2.at[i])
        arrived(w_at(far, bottom), yd2.at[i])

    lines = [-1, 1, 2]

    def line_start(j):
        ref = w_at(slot(lines[j], 0), YFIRST)
        send(ref, bs.at[j, 0], br.at[j, 1], at_z(1), tp)
        send(ref, bs.at[j, 1], bl.at[j, 1], at_z(-1), tp)

    def line(j, k):
        if k < 4:
            low, high = slot(lines[j], -k), slot(lines[j], k)
            arrived(w_at(low, YFIRST), br.at[j, k])
            part = YFIRST if k < 3 else halves(YFIRST)[0]
            send(w_at(low, part), bs.at[j, 2 * k], br.at[j, k + 1], at_z(1), tp)
            arrived(w_at(high, YFIRST), bl.at[j, k])
            part = YFIRST if k < 3 else halves(YFIRST)[1]
            send(w_at(high, part), bs.at[j, 2 * k + 1], bl.at[j, k + 1], at_z(-1), tp)
        else:
            far = slot(lines[j], 4)
            arrived(w_at(far, halves(YFIRST)[0]), br.at[j, 4])
            arrived(w_at(far, halves(YFIRST)[1]), bl.at[j, 4])

    def h_near():
        low, high = at_x(-1), at_x(1)
        arrived(hbuf.at[low], hx.at[0])
        h_sends.append(send(hbuf.at[low, pl.ds(0, 256), :], hxs.at[2], hx.at[2], st, at_x(1), False))
        h_sends.append(send(hbuf.at[low], hss.at[1], hs.at[1], st, sibling, False))
        arrived(hbuf.at[high], hx.at[1])
        h_sends.append(send(hbuf.at[high, pl.ds(256, 256), :], hxs.at[3], hx.at[3], st, at_x(-1), False))
        h_sends.append(send(hbuf.at[high], hss.at[2], hs.at[2], st, sibling, False))

    def h_far():
        far = at_x(2)
        arrived(hbuf.at[far, pl.ds(0, 256), :], hx.at[2])
        arrived(hbuf.at[far, pl.ds(256, 256), :], hx.at[3])
        h_sends.append(send(hbuf.at[far], hss.at[3], hs.at[3], st, sibling, False))

    def h_norm():
        for i, k in enumerate((0, -1, 1, 2)):
            piece = ((x + k + NX) % NX) * 2 + (1 - core)
            arrived(hbuf.at[piece], hs.at[i])
        for copy in h_sends:
            copy.wait_send()

        def block(b, carry):
            rows = pl.ds(pl.multiple_of(b * 32, 32), 32)
            total = jnp.zeros((32, 1), jnp.float32)
            for p in range(N_TP):
                raw = hbuf[p, rows, :].astype(jnp.float32)
                total += jnp.sum(raw * raw, axis=1, keepdims=True)
            scale = lax.rsqrt(total / (N_TP * FEATS) + 1e-05)
            for p in range(N_TP):
                raw = hbuf[p, rows, :].astype(jnp.float32)
                row_gain = gain[:, p * FEATS : (p + 1) * FEATS].astype(jnp.float32)
                hbuf[p, rows, :] = (raw * scale * row_gain).astype(jnp.bfloat16)
            return carry

        lax.fori_loop(0, SLOTS // 32, block, 0)

    acc[...] = jnp.zeros_like(acc)

    trickle()
    ring(1)
    trickle()
    y_near(0)
    trickle()
    line_start(0)
    line_start(1)
    ring(2)
    trickle()
    h_near()
    trickle()
    y_far(0)
    line_start(2)
    y_near(1)
    trickle()
    y_near(2)
    trickle()
    line(0, 1)
    line(1, 1)
    trickle()
    ring(3)
    trickle()
    h_far()
    y_near(3)
    trickle()
    y_near(4)
    trickle()
    line(2, 1)
    line(0, 2)
    trickle()
    line(1, 2)
    ring(4)
    trickle()
    h_norm()

    def project_row(dy):
        def step(i, carry):
            project(((y + dy + NY) % NY) * NZ + i)
            return carry

        lax.fori_loop(0, NZ, step, 0)

    y_near(5)
    trickle()
    y_near(6)
    trickle()
    line(2, 2)
    trickle()
    line(0, 3)
    trickle()
    line(1, 3)
    y_near(7)
    trickle()
    line(2, 3)
    for d in range(progress[1], N_STORE):
        stripe_start(d, 0)
    project_row(0)
    line(0, 4)
    line(1, 4)
    project_row(-1)
    project_row(1)
    line(2, 4)
    for i in range(1, 8):
        y_far(i)
    project_row(2)

    lane = lax.broadcasted_iota(jnp.int32, (TILE, HEAD), 1)
    frequency = jnp.exp((lane % (HEAD // 2)).astype(jnp.float32) * (-math.log(500000.0) * 2.0 / HEAD))
    for s in range(SLOTS // TILE):
        rows = slice(s * TILE, (s + 1) * TILE)
        position = lax.broadcasted_iota(jnp.int32, (TILE, HEAD), 0) + tiles[0, s] * TILE
        angle = position.astype(jnp.float32) * frequency
        cosine = jnp.cos(angle)
        sine = jnp.where(lane < HEAD // 2, -jnp.sin(angle), jnp.sin(angle))
        for h in range(5):
            vec = acc[rows, h * HEAD : (h + 1) * HEAD]
            turned = vec * cosine + pltpu.roll(vec, HEAD // 2, 1) * sine
            if h < 4:
                q_out[h, rows, :] = turned.astype(jnp.bfloat16)
            else:
                kv_out[rows, 0:HEAD] = turned.astype(jnp.bfloat16)
        kv_out[rows, HEAD : 2 * HEAD] = acc[rows, 5 * HEAD : 6 * HEAD].astype(jnp.bfloat16)

    def stripe_wait(d, carry):
        other = (st - d + N_STORE) % N_STORE
        arrived(inbox.at[other], pr.at[d])
        stripe_copy(d).wait_send()
        id_copy(d).wait_send()
        return carry

    lax.fori_loop(1, N_STORE, stripe_wait, 0)
    own_stripes.wait()
    for copy in pending:
        copy.wait_send()


def exchange(hidden, gain, wq, km, vm, cache, ids, tiles):
    any_space = pl.BlockSpec(memory_space=pl.ANY)
    vmem = pl.BlockSpec(memory_space=pltpu.VMEM)
    smem = pl.BlockSpec(memory_space=pltpu.SMEM)
    dma = pltpu.SemaphoreType.DMA
    return pl.pallas_call(
        exchange_kernel,
        out_shape=[
            jax.ShapeDtypeStruct((4, SLOTS, HEAD), jnp.bfloat16),
            jax.ShapeDtypeStruct((SLOTS, 2 * HEAD), jnp.bfloat16),
            jax.ShapeDtypeStruct((N_STORE, PASSAGES * STRIPE, 2 * HEAD), jnp.bfloat16),
        ],
        in_specs=[any_space, vmem, any_space, any_space, any_space, any_space, vmem, smem],
        out_specs=[vmem, vmem, any_space],
        scratch_shapes=[
            pltpu.VMEM((N_TP, SLOTS, FEATS), jnp.bfloat16),
            pltpu.VMEM((N_STORE, CHUNK, COLS), jnp.bfloat16),
            pltpu.VMEM((128, STRIPE, 2 * HEAD), jnp.bfloat16),
            pltpu.VMEM((N_STORE, PASSAGES * STRIPE, 2 * HEAD), jnp.bfloat16),
            pltpu.VMEM((1, 128), jnp.int32),
            pltpu.VMEM((N_STORE, 1, 128), jnp.int32),
            pltpu.SMEM((N_STORE, 1, 128), jnp.int32),
            pltpu.VMEM((SLOTS, COLS), jnp.float32),
            dma((5,)),
            dma((5,)), dma((5,)), dma((8,)), dma((8,)), dma((8,)), dma((8,)),
            dma((3, 5)), dma((3, 5)), dma((4,)), dma((4,)), dma((32,)), dma((32,)),
            dma((8,)), dma((16,)), dma((16,)), dma((3, 8)), dma((4,)), dma((4,)), dma((32,)), dma((32,)),
        ],
        compiler_params=pltpu.CompilerParams(
            collective_id=0, has_side_effects=True, vmem_limit_bytes=62 * 2**20
        ),
    )(hidden, gain, wq, km, vm, cache, ids, tiles)


KEYS = 512


def attend_kernel(ids, placement, tiles, count, q, kv, inbox, out, context, scores, highest, total, values):
    for j in range(PASSAGES):
        turn = placement[ids[0, j]]

        def order(i, carry):
            source = (i - turn + N_STORE) % N_STORE
            rows = pl.ds(pl.multiple_of(j * 1024 + i * STRIPE, STRIPE), STRIPE)
            context[rows, :] = inbox[source, j * STRIPE : (j + 1) * STRIPE, :]
            return carry

        lax.fori_loop(0, N_STORE, order, 0)
    for s in range(SLOTS // TILE):
        @pl.when(s < count[0])
        def _():
            rows = pl.ds(pl.multiple_of(tiles[0, s] * TILE, TILE), TILE)
            context[rows, :] = kv[s * TILE : (s + 1) * TILE, :]

    def one_slot(s, carry):
        slot_rows = pl.ds(pl.multiple_of(s * TILE, TILE), TILE)

        @pl.when(s >= count[0])
        def _():
            out[slot_rows, :] = jnp.zeros((TILE, 4 * HEAD), jnp.bfloat16)

        @pl.when(s < count[0])
        def _():
            tile = tiles[0, s]
            last = tile // (KEYS // TILE)
            query = q[:, slot_rows, :].reshape(4 * TILE, HEAD)

            def block_scores(b):
                keys = context[pl.ds(pl.multiple_of(b * KEYS, KEYS), KEYS), 0:HEAD]
                return lax.dot_general(
                    query, keys, (((1,), (1,)), ((), ())), preferred_element_type=jnp.float32
                )

            def widest(block):
                top = block[:, 0:HEAD]
                for n in range(1, KEYS // HEAD):
                    top = jnp.maximum(top, block[:, n * HEAD : (n + 1) * HEAD])
                return top

            block = block_scores(last)
            row = lax.broadcasted_iota(jnp.int32, (4 * TILE, KEYS), 0) % TILE + tile * TILE
            column = lax.broadcasted_iota(jnp.int32, (4 * TILE, KEYS), 1) + last * KEYS
            block = jnp.where(column <= row, block, -jnp.inf)
            scores[last] = block
            highest[...] = widest(block)

            def first_pass(b, carry):
                block = block_scores(b)
                scores[b] = block
                highest[...] = jnp.maximum(highest[...], widest(block))
                return carry

            lax.fori_loop(0, last, first_pass, 0)
            shift = jnp.max(highest[...], axis=1, keepdims=True) * SCORE
            total[...] = jnp.zeros_like(total)
            values[...] = jnp.zeros_like(values)

            def second_pass(b, carry):
                terms = jnp.exp2(scores[b] * SCORE - shift)
                part = terms[:, 0:HEAD]
                for n in range(1, KEYS // HEAD):
                    part = part + terms[:, n * HEAD : (n + 1) * HEAD]
                total[...] += part
                rows = pl.ds(pl.multiple_of(b * KEYS, KEYS), KEYS)
                values[...] += jnp.dot(
                    terms.astype(jnp.bfloat16), context[rows, HEAD : 2 * HEAD],
                    preferred_element_type=jnp.float32,
                )
                return carry

            lax.fori_loop(0, last + 1, second_pass, 0)
            result = values[...] / jnp.sum(total[...], axis=1, keepdims=True)
            for h in range(4):
                out[slot_rows, h * HEAD : (h + 1) * HEAD] = result[h * TILE : (h + 1) * TILE, :].astype(
                    jnp.bfloat16
                )

        return carry

    lax.fori_loop(0, SLOTS // TILE, one_slot, 0)


def attend(ids, placement, tiles, count, q, kv, inbox):
    vmem = pl.BlockSpec(memory_space=pltpu.VMEM)
    smem = pl.BlockSpec(memory_space=pltpu.SMEM)
    return pl.pallas_call(
        attend_kernel,
        out_shape=jax.ShapeDtypeStruct((SLOTS, 4 * HEAD), jnp.bfloat16),
        in_specs=[smem, smem, smem, smem, vmem, vmem, vmem],
        out_specs=vmem,
        scratch_shapes=[
            pltpu.VMEM((PASSAGES * 1024, 2 * HEAD), jnp.bfloat16),
            pltpu.VMEM((PASSAGES * 1024 // KEYS, 4 * TILE, KEYS), jnp.float32),
            pltpu.VMEM((4 * TILE, HEAD), jnp.float32),
            pltpu.VMEM((4 * TILE, HEAD), jnp.float32),
            pltpu.VMEM((4 * TILE, HEAD), jnp.float32),
        ],
        compiler_params=pltpu.CompilerParams(vmem_limit_bytes=62 * 2**20),
    )(ids, placement, tiles, count, q, kv, inbox)


def local(hidden, gain, w_query, key_matrix, value_matrix, passage_cache, passage_ids, placement, tile_index, tile_count):
    q, kv, inbox = exchange(
        hidden, gain.reshape(1, -1), w_query, key_matrix, value_matrix, passage_cache, passage_ids, tile_index
    )
    return attend(passage_ids, placement, tile_index, tile_count, q, kv, inbox)


def solution(mesh):
    placed = (
        P("store", "tp"), P(), P("store", "tp"), P("store", "tp"), P("store", "tp"),
        P(None, "store", "tp"), P("store", None), P(), P("store", None), P("store"),
    )
    return jax.shard_map(local, mesh=mesh, in_specs=placed, out_specs=P("store", "tp"), check_vma=False)
```

```python
import math

import jax
import jax.numpy as jnp
from jax import lax
from jax.experimental import pallas as pl
from jax.experimental.pallas import tpu as pltpu
from jax.sharding import PartitionSpec as P

HEAD = 128
NY, NZ, NX = 4, 8, 4
N_STORE = NY * NZ
N_TP = 2 * NX
SLOTS = 512
TILE = 128
PASSAGES = 6
STRIPE = 32
CHUNK = 256
COLS = 768
FEATS = 1024
KEEP = 192
FULL = (0, CHUNK)
ZFIRST = (0, KEEP)
YFIRST = (KEEP, CHUNK)
MESH_ID = pl.DeviceIdType.MESH
SCORE = math.log2(math.e) / math.sqrt(HEAD)


def halves(rows):
    low, high = rows
    middle = (low + high) // 2
    return (low, middle), (middle, high)


def exchange_kernel(
    hidden, gain, wq, km, vm, cache, ids, tiles,
    q_out, kv_out, inbox,
    hbuf, wbuf, cbuf, outbox, idrow, idbuf, idmem, acc, turn,
    load_sem, zr, zl, yu, yd, yu2, yd2, br, bl, hx, hs, idr, pr,
    zs, ys, ys2, bs, hxs, hss, ids_s, ps,
):
    st = lax.axis_index("store")
    tp = lax.axis_index("tp")
    y, z = st // NZ, st % NZ
    x, core = tp // 2, tp % 2
    sibling = x * 2 + (1 - core)

    def at_z(k):
        return y * NZ + (z + k + NZ) % NZ

    def at_y(k):
        return ((y + k + NY) % NY) * NZ + z

    def slot(dy, dz):
        return ((y + dy + NY) % NY) * NZ + (z + dz + NZ) % NZ

    def at_x(k):
        return ((x + k + NX) % NX) * 2 + core

    loads = [
        pltpu.make_async_copy(wq, wbuf.at[st, :, pl.ds(0, 512)], load_sem.at[0]),
        pltpu.make_async_copy(km, wbuf.at[st, :, pl.ds(512, 128)], load_sem.at[1]),
        pltpu.make_async_copy(vm, wbuf.at[st, :, pl.ds(640, 128)], load_sem.at[2]),
        pltpu.make_async_copy(hidden, hbuf.at[tp], load_sem.at[3]),
        pltpu.make_async_copy(cache, cbuf, load_sem.at[4]),
    ]
    for load in loads:
        load.start()
    idrow[...] = jnp.zeros_like(idrow)
    idrow[0:1, 0:PASSAGES] = ids[...]

    barrier = pltpu.get_barrier_semaphore()

    def greet(d, carry):
        pl.semaphore_signal(
            barrier, inc=1, device_id=((st + d) % N_STORE, tp), device_id_type=MESH_ID
        )
        return carry

    lax.fori_loop(1, N_STORE, greet, 0)
    for peer in (at_x(1), at_x(-1), sibling):
        pl.semaphore_signal(barrier, inc=1, device_id=(st, peer), device_id_type=MESH_ID)
    pl.semaphore_wait(barrier, N_STORE - 1 + 3)

    pending = []

    def send(ref, send_sem, recv_sem, store, peer, later=True):
        copy = pltpu.make_async_remote_copy(
            src_ref=ref, dst_ref=ref, send_sem=send_sem, recv_sem=recv_sem,
            device_id=(store, peer), device_id_type=MESH_ID,
        )
        copy.start()
        if later:
            pending.append(copy)
        return copy

    def arrived(ref, sem):
        pltpu.make_async_copy(ref, ref, sem).wait()

    def w_at(chunk, rows):
        return wbuf.at[chunk, pl.ds(rows[0], rows[1] - rows[0]), :]

    def id_copy(d):
        other = (st + d) % N_STORE
        return pltpu.make_async_remote_copy(
            src_ref=idrow, dst_ref=idbuf.at[st], send_sem=ids_s.at[d], recv_sem=idr.at[d],
            device_id=(other, tp), device_id_type=MESH_ID,
        )

    def id_start(d, carry):
        id_copy(d).start()
        return carry

    lax.fori_loop(1, N_STORE, id_start, 0)

    for load in loads:
        load.wait()
    own = w_at(st, FULL)
    send(own, zs.at[0], zr.at[1], at_z(1), tp)
    send(own, zs.at[1], zl.at[1], at_z(-1), tp)
    send(own, ys.at[0], yu.at[0], at_y(1), tp)
    send(own, ys.at[1], yd.at[0], at_y(-1), tp)
    h_sends = []
    h_own = hbuf.at[tp]
    h_sends.append(send(h_own, hxs.at[0], hx.at[0], st, at_x(1), False))
    h_sends.append(send(h_own, hxs.at[1], hx.at[1], st, at_x(-1), False))
    h_sends.append(send(h_own, hss.at[0], hs.at[0], st, sibling, False))

    idbuf[pl.ds(st, 1), :, :] = idrow[...].reshape(1, 1, 128)

    def id_wait(d, carry):
        other = (st - d + N_STORE) % N_STORE
        arrived(idbuf.at[other], idr.at[d])
        return carry

    lax.fori_loop(1, N_STORE, id_wait, 0)
    to_scalar = pltpu.make_async_copy(idbuf, idmem, load_sem.at[0])
    to_scalar.start()
    to_scalar.wait()

    def stripe_copy(d):
        other = (st + d) % N_STORE
        return pltpu.make_async_remote_copy(
            src_ref=outbox.at[other], dst_ref=inbox.at[st], send_sem=ps.at[d], recv_sem=pr.at[d],
            device_id=(other, tp), device_id_type=MESH_ID,
        )

    def fill(other):
        for j in range(PASSAGES):
            outbox[other, j * STRIPE : (j + 1) * STRIPE, :] = cbuf[idmem[other, 0, j]]

    def stripe_start(d, carry):
        fill((st + d) % N_STORE)
        stripe_copy(d).start()
        return carry

    fill(st)
    own_stripes = pltpu.make_async_copy(outbox.at[st], inbox.at[st], load_sem.at[1])
    own_stripes.start()

    progress = [0, 1]

    def trickle():
        progress[0] += 1
        if progress[0] > 4:
            stop = min(N_STORE, progress[1] + 2)
            for d in range(progress[1], stop):
                stripe_start(d, 0)
            progress[1] = stop

    def project(chunk):
        piece = chunk // 4
        column = pl.multiple_of((chunk % 4) * CHUNK, CHUNK)
        for m in range(2):
            rows = slice(m * 256, (m + 1) * 256)
            acc[rows, :] += jnp.dot(
                hbuf[piece, rows, pl.ds(column, CHUNK)], wbuf[chunk], preferred_element_type=jnp.float32
            )

    offsets = [0, -1, 1, -2, 2, -3, 3, 4]

    def forward_y(i):
        ref = w_at(slot(0, offsets[i]), ZFIRST)
        send(ref, ys.at[2 * i], yu.at[i], at_y(1), tp)
        send(ref, ys.at[2 * i + 1], yd.at[i], at_y(-1), tp)

    def ring(k):
        if k < 4:
            low, high = slot(0, -k), slot(0, k)
            arrived(w_at(low, FULL), zr.at[k])
            part = FULL if k < 3 else halves(FULL)[0]
            send(w_at(low, part), zs.at[2 * k], zr.at[k + 1], at_z(1), tp)
            arrived(w_at(high, FULL), zl.at[k])
            part = FULL if k < 3 else halves(FULL)[1]
            send(w_at(high, part), zs.at[2 * k + 1], zl.at[k + 1], at_z(-1), tp)
            forward_y(2 * k - 1)
            forward_y(2 * k)
        else:
            far = slot(0, 4)
            arrived(w_at(far, halves(FULL)[0]), zr.at[4])
            arrived(w_at(far, halves(FULL)[1]), zl.at[4])
            forward_y(7)

    def y_near(i):
        rows = FULL if i == 0 else ZFIRST
        top, bottom = halves(rows)
        below, above = slot(-1, offsets[i]), slot(1, offsets[i])
        arrived(w_at(below, rows), yu.at[i])
        send(w_at(below, top), ys2.at[2 * i], yu2.at[i], at_y(1), tp)
        arrived(w_at(above, rows), yd.at[i])
        send(w_at(above, bottom), ys2.at[2 * i + 1], yd2.at[i], at_y(-1), tp)

    def y_far(i):
        rows = FULL if i == 0 else ZFIRST
        top, bottom = halves(rows)
        far = slot(2, offsets[i])
        arrived(w_at(far, top), yu2.at[i])
        arrived(w_at(far, bottom), yd2.at[i])

    lines = [-1, 1, 2]

    def line_start(j):
        ref = w_at(slot(lines[j], 0), YFIRST)
        send(ref, bs.at[j, 0], br.at[j, 1], at_z(1), tp)
        send(ref, bs.at[j, 1], bl.at[j, 1], at_z(-1), tp)

    def line(j, k):
        if k < 4:
            low, high = slot(lines[j], -k), slot(lines[j], k)
            arrived(w_at(low, YFIRST), br.at[j, k])
            part = YFIRST if k < 3 else halves(YFIRST)[0]
            send(w_at(low, part), bs.at[j, 2 * k], br.at[j, k + 1], at_z(1), tp)
            arrived(w_at(high, YFIRST), bl.at[j, k])
            part = YFIRST if k < 3 else halves(YFIRST)[1]
            send(w_at(high, part), bs.at[j, 2 * k + 1], bl.at[j, k + 1], at_z(-1), tp)
        else:
            far = slot(lines[j], 4)
            arrived(w_at(far, halves(YFIRST)[0]), br.at[j, 4])
            arrived(w_at(far, halves(YFIRST)[1]), bl.at[j, 4])

    def h_near():
        low, high = at_x(-1), at_x(1)
        arrived(hbuf.at[low], hx.at[0])
        h_sends.append(send(hbuf.at[low, pl.ds(0, 256), :], hxs.at[2], hx.at[2], st, at_x(1), False))
        h_sends.append(send(hbuf.at[low], hss.at[1], hs.at[1], st, sibling, False))
        arrived(hbuf.at[high], hx.at[1])
        h_sends.append(send(hbuf.at[high, pl.ds(256, 256), :], hxs.at[3], hx.at[3], st, at_x(-1), False))
        h_sends.append(send(hbuf.at[high], hss.at[2], hs.at[2], st, sibling, False))

    def h_far():
        far = at_x(2)
        arrived(hbuf.at[far, pl.ds(0, 256), :], hx.at[2])
        arrived(hbuf.at[far, pl.ds(256, 256), :], hx.at[3])
        h_sends.append(send(hbuf.at[far], hss.at[3], hs.at[3], st, sibling, False))

    def h_norm():
        for i, k in enumerate((0, -1, 1, 2)):
            piece = ((x + k + NX) % NX) * 2 + (1 - core)
            arrived(hbuf.at[piece], hs.at[i])
        for copy in h_sends:
            copy.wait_send()

        def block(b, carry):
            rows = pl.ds(pl.multiple_of(b * 32, 32), 32)
            total = jnp.zeros((32, 1), jnp.float32)
            for p in range(N_TP):
                raw = hbuf[p, rows, :].astype(jnp.float32)
                total += jnp.sum(raw * raw, axis=1, keepdims=True)
            scale = lax.rsqrt(total / (N_TP * FEATS) + 1e-05)
            for p in range(N_TP):
                raw = hbuf[p, rows, :].astype(jnp.float32)
                row_gain = gain[p * FEATS : (p + 1) * FEATS].astype(jnp.float32).reshape(1, FEATS)
                hbuf[p, rows, :] = (raw * scale * row_gain).astype(jnp.bfloat16)
            return carry

        lax.fori_loop(0, SLOTS // 32, block, 0)

    acc[...] = jnp.zeros_like(acc)

    trickle()
    ring(1)
    trickle()
    y_near(0)
    trickle()
    line_start(0)
    line_start(1)
    ring(2)
    trickle()
    h_near()
    trickle()
    y_far(0)
    line_start(2)
    y_near(1)
    trickle()
    y_near(2)
    trickle()
    line(0, 1)
    line(1, 1)
    trickle()
    ring(3)
    trickle()
    h_far()
    y_near(3)
    trickle()
    y_near(4)
    trickle()
    line(2, 1)
    line(0, 2)
    trickle()
    line(1, 2)
    ring(4)
    trickle()
    h_norm()

    lane = lax.broadcasted_iota(jnp.int32, (TILE, HEAD), 1)
    frequency = jnp.exp((lane % (HEAD // 2)).astype(jnp.float32) * (-math.log(500000.0) * 2.0 / HEAD))
    for s in range(SLOTS // TILE):
        position = lax.broadcasted_iota(jnp.int32, (TILE, HEAD), 0) + tiles[0, s] * TILE
        angle = position.astype(jnp.float32) * frequency
        turn[0, s] = jnp.cos(angle)
        turn[1, s] = jnp.where(lane < HEAD // 2, -jnp.sin(angle), jnp.sin(angle))

    def project_row(dy):
        def step(i, carry):
            project(((y + dy + NY) % NY) * NZ + i)
            return carry

        lax.fori_loop(0, NZ, step, 0)

    y_near(5)
    trickle()
    y_near(6)
    trickle()
    line(2, 2)
    trickle()
    line(0, 3)
    trickle()
    line(1, 3)
    y_near(7)
    trickle()
    line(2, 3)
    for d in range(progress[1], N_STORE):
        stripe_start(d, 0)
    project_row(0)
    line(0, 4)
    line(1, 4)
    project_row(-1)
    project_row(1)
    line(2, 4)
    project(slot(2, 0))

    def far_step(i, carry):
        offset = ((i + 1) // 2) * (1 - 2 * (i % 2))
        chunk = ((y + 2) % NY) * NZ + (z + offset + NZ) % NZ
        top_rows, bottom_rows = halves(ZFIRST)
        arrived(w_at(chunk, top_rows), yu2.at[i])
        arrived(w_at(chunk, bottom_rows), yd2.at[i])
        project(chunk)
        return carry

    lax.fori_loop(1, NZ, far_step, 0)

    for s in range(SLOTS // TILE):
        rows = slice(s * TILE, (s + 1) * TILE)
        for h in range(5):
            vec = acc[rows, h * HEAD : (h + 1) * HEAD]
            turned = vec * turn[0, s] + pltpu.roll(vec, HEAD // 2, 1) * turn[1, s]
            if h < 4:
                q_out[h, rows, :] = turned.astype(jnp.bfloat16)
            else:
                kv_out[rows, 0:HEAD] = turned.astype(jnp.bfloat16)
        kv_out[rows, HEAD : 2 * HEAD] = acc[rows, 5 * HEAD : 6 * HEAD].astype(jnp.bfloat16)

    def stripe_wait(d, carry):
        other = (st - d + N_STORE) % N_STORE
        arrived(inbox.at[other], pr.at[d])
        stripe_copy(d).wait_send()
        id_copy(d).wait_send()
        return carry

    lax.fori_loop(1, N_STORE, stripe_wait, 0)
    own_stripes.wait()
    for copy in pending:
        copy.wait_send()


def exchange(hidden, gain, wq, km, vm, cache, ids, tiles):
    any_space = pl.BlockSpec(memory_space=pl.ANY)
    vmem = pl.BlockSpec(memory_space=pltpu.VMEM)
    smem = pl.BlockSpec(memory_space=pltpu.SMEM)
    dma = pltpu.SemaphoreType.DMA
    return pl.pallas_call(
        exchange_kernel,
        out_shape=[
            jax.ShapeDtypeStruct((4, SLOTS, HEAD), jnp.bfloat16),
            jax.ShapeDtypeStruct((SLOTS, 2 * HEAD), jnp.bfloat16),
            jax.ShapeDtypeStruct((N_STORE, PASSAGES * STRIPE, 2 * HEAD), jnp.bfloat16),
        ],
        in_specs=[any_space, vmem, any_space, any_space, any_space, any_space, vmem, smem],
        out_specs=[vmem, vmem, any_space],
        scratch_shapes=[
            pltpu.VMEM((N_TP, SLOTS, FEATS), jnp.bfloat16),
            pltpu.VMEM((N_STORE, CHUNK, COLS), jnp.bfloat16),
            pltpu.VMEM((128, STRIPE, 2 * HEAD), jnp.bfloat16),
            pltpu.VMEM((N_STORE, PASSAGES * STRIPE, 2 * HEAD), jnp.bfloat16),
            pltpu.VMEM((1, 128), jnp.int32),
            pltpu.VMEM((N_STORE, 1, 128), jnp.int32),
            pltpu.SMEM((N_STORE, 1, 128), jnp.int32),
            pltpu.VMEM((SLOTS, COLS), jnp.float32),
            pltpu.VMEM((2, 4, TILE, HEAD), jnp.float32),
            dma((5,)),
            dma((5,)), dma((5,)), dma((8,)), dma((8,)), dma((8,)), dma((8,)),
            dma((3, 5)), dma((3, 5)), dma((4,)), dma((4,)), dma((32,)), dma((32,)),
            dma((8,)), dma((16,)), dma((16,)), dma((3, 8)), dma((4,)), dma((4,)), dma((32,)), dma((32,)),
        ],
        compiler_params=pltpu.CompilerParams(
            collective_id=0, has_side_effects=True, vmem_limit_bytes=62 * 2**20
        ),
    )(hidden, gain, wq, km, vm, cache, ids, tiles)


KEYS = 1024
STR = KEYS // STRIPE
PER = 1024 // KEYS


def attend_kernel(ids, placement, tiles, count, q, kv, inbox, out, stripes, scores, highest, total, values, sem):
    load = pltpu.make_async_copy(inbox, stripes, sem)
    load.start()
    load.wait()

    def block_of(b, lanes):
        j = b // PER
        first = b % PER * STR + N_STORE - placement[ids[0, j]]
        rows = pl.ds(pl.multiple_of(j * STRIPE, STRIPE), STRIPE)
        return jnp.concatenate([stripes[(first + k) % N_STORE, rows, lanes] for k in range(STR)], axis=0)

    for s in range(SLOTS // TILE):
        @pl.when(s < count[0])
        def _():
            j = tiles[0, s] // 8
            first = tiles[0, s] % 8 * 4 + N_STORE - placement[ids[0, j]]
            rows = pl.ds(pl.multiple_of(j * STRIPE, STRIPE), STRIPE)
            for k in range(4):
                part = s * TILE + k * STRIPE
                stripes[(first + k) % N_STORE, rows, :] = kv[part : part + STRIPE, :]

    def one_slot(s, carry):
        slot_rows = pl.ds(pl.multiple_of(s * TILE, TILE), TILE)

        @pl.when(s >= count[0])
        def _():
            out[slot_rows, :] = jnp.zeros((TILE, 4 * HEAD), jnp.bfloat16)

        @pl.when(s < count[0])
        def _():
            tile = tiles[0, s]
            last = tile // (KEYS // TILE)
            query = q[:, slot_rows, :].reshape(4 * TILE, HEAD)

            def block_scores(b):
                return lax.dot_general(
                    query, block_of(b, slice(0, HEAD)), (((1,), (1,)), ((), ())), preferred_element_type=jnp.float32
                )

            def widest(block):
                top = block[:, 0:HEAD]
                for n in range(1, KEYS // HEAD):
                    top = jnp.maximum(top, block[:, n * HEAD : (n + 1) * HEAD])
                return top

            block = block_scores(last)
            row = lax.broadcasted_iota(jnp.int32, (4 * TILE, KEYS), 0) % TILE + tile * TILE
            column = lax.broadcasted_iota(jnp.int32, (4 * TILE, KEYS), 1) + last * KEYS
            block = jnp.where(column <= row, block, -jnp.inf)
            scores[last] = block
            highest[...] = widest(block)

            def first_step(b):
                block = block_scores(b)
                scores[b] = block
                highest[...] = jnp.maximum(highest[...], widest(block))

            def second_step(b):
                terms = jnp.exp2(scores[b] * SCORE - shift)
                part = terms[:, 0:HEAD]
                for n in range(1, KEYS // HEAD):
                    part = part + terms[:, n * HEAD : (n + 1) * HEAD]
                total[...] += part
                values[...] += jnp.dot(
                    terms.astype(jnp.bfloat16), block_of(b, slice(HEAD, 2 * HEAD)), preferred_element_type=jnp.float32
                )

            def over(step, n):
                def pair(i, carry):
                    step(2 * i)
                    step(2 * i + 1)
                    return carry

                lax.fori_loop(0, n // 2, pair, 0)

                @pl.when(n % 2 == 1)
                def _():
                    step(n - 1)

            over(first_step, last)
            shift = jnp.max(highest[...], axis=1, keepdims=True) * SCORE
            total[...] = jnp.zeros_like(total)
            values[...] = jnp.zeros_like(values)
            over(second_step, last + 1)
            result = values[...] / jnp.sum(total[...], axis=1, keepdims=True)
            for h in range(4):
                out[slot_rows, h * HEAD : (h + 1) * HEAD] = result[h * TILE : (h + 1) * TILE, :].astype(jnp.bfloat16)

        return carry

    lax.fori_loop(0, SLOTS // TILE, one_slot, 0)

def attend(ids, placement, tiles, count, q, kv, inbox):
    vmem = pl.BlockSpec(memory_space=pltpu.VMEM)
    smem = pl.BlockSpec(memory_space=pltpu.SMEM)
    return pl.pallas_call(
        attend_kernel,
        out_shape=jax.ShapeDtypeStruct((SLOTS, 4 * HEAD), jnp.bfloat16),
        in_specs=[smem, smem, smem, smem, vmem, vmem, pl.BlockSpec(memory_space=pl.ANY)],
        out_specs=vmem,
        scratch_shapes=[
            pltpu.VMEM((N_STORE, PASSAGES * STRIPE, 2 * HEAD), jnp.bfloat16),
            pltpu.VMEM((PASSAGES * 1024 // KEYS, 4 * TILE, KEYS), jnp.float32),
            pltpu.VMEM((4 * TILE, HEAD), jnp.float32),
            pltpu.VMEM((4 * TILE, HEAD), jnp.float32),
            pltpu.VMEM((4 * TILE, HEAD), jnp.float32),
            pltpu.SemaphoreType.DMA,
        ],
        compiler_params=pltpu.CompilerParams(vmem_limit_bytes=62 * 2**20),
    )(ids, placement, tiles, count, q, kv, inbox)


def local(hidden, gain, w_query, key_matrix, value_matrix, passage_cache, passage_ids, placement, tile_index, tile_count):
    q, kv, inbox = exchange(
        hidden, gain, w_query, key_matrix, value_matrix, passage_cache, passage_ids, tile_index
    )
    return attend(passage_ids, placement, tile_index, tile_count, q, kv, inbox)


def solution(mesh):
    placed = (
        P("store", "tp"), P(), P("store", "tp"), P("store", "tp"), P("store", "tp"),
        P(None, "store", "tp"), P("store", None), P(), P("store", None), P("store"),
    )
    return jax.shard_map(local, mesh=mesh, in_specs=placed, out_specs=P("store", "tp"), check_vma=False)
```

```python
import math

import jax
import jax.numpy as jnp
from jax import lax
from jax.experimental import pallas as pl
from jax.experimental.pallas import tpu as pltpu
from jax.sharding import PartitionSpec as P

HEAD = 128
NY, NZ, NX = 4, 8, 4
N_STORE = NY * NZ
N_TP = 2 * NX
SLOTS = 512
TILE = 128
PASSAGES = 6
STRIPE = 32
CHUNK = 256
COLS = 768
FEATS = 1024
TRS = 7
TRN = 3
KEEP = 224
FULL = (0, CHUNK)
ZFIRST = (0, KEEP)
YFIRST = (KEEP, CHUNK)
MESH_ID = pl.DeviceIdType.MESH
SCORE = math.log2(math.e) / math.sqrt(HEAD)


def halves(rows):
    low, high = rows
    middle = (low + high) // 2
    return (low, middle), (middle, high)


def exchange_kernel(
    hidden, gain, wq, km, vm, cache, ids, tiles,
    q_out, kv_out, inbox,
    hown, hbuf, wbuf, cbuf, outbox, idrow, idbuf, idmem, acc, turn, squares, squares_in, partial, partial_in,
    load_sem, zr, zl, yo, br, bl, hp, hn, hf, hs, idr, pr, sr,
    zs, ys, bs, hps, hns, hfs, hss, ids_s, ps, ss,
):
    st = lax.axis_index("store")
    tp = lax.axis_index("tp")
    y, z = st // NZ, st % NZ
    x, core = tp // 2, tp % 2

    def partner_of(i):
        return i + 1 - 2 * (i % 2)

    def across_from(i):
        return (i + 3 + 2 * (i % 2)) % 4

    y_partner, y_across = partner_of(y), across_from(y)
    x_partner, x_across = partner_of(x) * 2 + core, across_from(x) * 2 + core
    sibling = x * 2 + (1 - core)
    st_partner, st_across = y_partner * NZ + z, y_across * NZ + z
    is_source = (x == y) | (x == y_across)
    near = jnp.where((x == y) | (partner_of(x) == y), 0, 1)
    far = 1 - near

    def piece_at(token, side, c):
        return token * 4 + side * 2 + c

    def at_z(k):
        return y * NZ + (z + k + NZ) % NZ

    def slot(side, dz):
        return side * NZ + (z + dz + NZ) % NZ

    loads = [
        pltpu.make_async_copy(wq, wbuf.at[z, :, pl.ds(0, 512)], load_sem.at[0]),
        pltpu.make_async_copy(km, wbuf.at[z, :, pl.ds(512, 128)], load_sem.at[1]),
        pltpu.make_async_copy(vm, wbuf.at[z, :, pl.ds(640, 128)], load_sem.at[2]),
        pltpu.make_async_copy(hidden, hown, load_sem.at[3]),
        pltpu.make_async_copy(cache, cbuf, load_sem.at[4]),
    ]
    for load in loads:
        load.start()
    idrow[...] = jnp.zeros_like(idrow)
    idrow[0:1, 0:PASSAGES] = ids[...]

    barrier = pltpu.get_barrier_semaphore()

    def greet(d, carry):
        pl.semaphore_signal(
            barrier, inc=1, device_id=((st + d) % N_STORE, tp), device_id_type=MESH_ID
        )
        return carry

    lax.fori_loop(1, N_STORE, greet, 0)
    for peer in (x_partner, x_across, sibling):
        pl.semaphore_signal(barrier, inc=1, device_id=(st, peer), device_id_type=MESH_ID)
    pl.semaphore_wait(barrier, N_STORE - 1 + 3)

    pending = []

    def move(src, dst, send_sem, recv_sem, store, peer):
        return pltpu.make_async_remote_copy(
            src_ref=src, dst_ref=dst, send_sem=send_sem, recv_sem=recv_sem,
            device_id=(store, peer), device_id_type=MESH_ID,
        )

    def send(src, dst, send_sem, recv_sem, store, peer, sends=pending):
        copy = move(src, dst, send_sem, recv_sem, store, peer)
        copy.start()
        sends.append(copy)

    def arrived(ref, sem):
        pltpu.make_async_copy(ref, ref, sem).wait()

    def w_at(chunk, rows):
        return wbuf.at[chunk, pl.ds(rows[0], rows[1] - rows[0]), :]

    def id_copy(d):
        other = (st + d) % N_STORE
        return move(idrow, idbuf.at[st], ids_s.at[d], idr.at[d], other, tp)

    def id_start(d, carry):
        id_copy(d).start()
        return carry

    lax.fori_loop(1, N_STORE, id_start, 0)

    for load in loads:
        load.wait()

    def send_w(chunk, to, rows, send_sem, recv_sem, store):
        send(w_at(chunk, rows), w_at(to, rows), send_sem, recv_sem, store, tp)

    send_w(z, z, FULL, zs.at[0], zr.at[1], at_z(1))
    send_w(z, z, FULL, zs.at[1], zl.at[1], at_z(-1))
    send_w(z, NZ + z, FULL, ys.at[0], yo.at[0], st_across)

    h_sends = []
    own_piece = piece_at(0, near, core)
    keep = pltpu.make_async_copy(hown, hbuf.at[own_piece], load_sem.at[0])
    partner_piece = piece_at(1, jnp.where(x == y_partner, 0, 1), core)

    def half(piece, part):
        return hbuf.at[piece, pl.ds(part * 256, 256), :]

    def to_partner(part):
        return move(
            hown.at[pl.ds(part * 256, 256), :], half(partner_piece, part), hps.at[part], hp.at[part], st_partner, tp
        )

    def h_to_near(token, part):
        ref, n = half(piece_at(token, near, core), part), 2 * token + part
        return move(ref, ref, hns.at[n], hn.at[n], st, x_partner)

    def h_pass(token, part):
        ref, n = half(piece_at(token, near, core), part), 2 * token + part
        return [
            move(ref, ref, hfs.at[n], hf.at[n], st, x_across),
            move(ref, ref, hss.at[n], hs.at[n], st, sibling),
        ]

    def h_far(token, part):
        ref, n = half(piece_at(token, far, core), part), 2 * token + part
        arrived(ref, hf.at[n])
        send(ref, ref, hss.at[4 + n], hs.at[4 + n], st, sibling, h_sends)

    def source_pass(token, part):
        h_to_near(token, part).start()
        for copy in h_pass(token, part):
            copy.start()

    def source_step(part):
        @pl.when(is_source)
        def _():
            arrived(half(piece_at(1, near, core), part), hp.at[part])
            source_pass(1, part)

    def other_step(token, part):
        @pl.when(jnp.logical_not(is_source))
        def _():
            arrived(half(piece_at(token, near, core), part), hn.at[2 * token + part])
            for copy in h_pass(token, part):
                copy.start()

    @pl.when(is_source)
    def _():
        keep.start()
        keep.wait()
        for part in range(2):
            source_pass(0, part)

    @pl.when(jnp.logical_not(is_source))
    def _():
        for part in range(2):
            to_partner(part).start()

    idbuf[pl.ds(st, 1), :, :] = idrow[...].reshape(1, 1, 128)

    def id_wait(d, carry):
        other = (st - d + N_STORE) % N_STORE
        arrived(idbuf.at[other], idr.at[d])
        return carry

    lax.fori_loop(1, N_STORE, id_wait, 0)
    to_scalar = pltpu.make_async_copy(idbuf, idmem, load_sem.at[0])
    to_scalar.start()
    to_scalar.wait()

    def stripe_copy(d):
        other = (st + d) % N_STORE
        return move(outbox.at[other], inbox.at[st], ps.at[d], pr.at[d], other, tp)

    def fill(other):
        for j in range(PASSAGES):
            outbox[other, j * STRIPE : (j + 1) * STRIPE, :] = cbuf[idmem[other, 0, j]]

    fill(st)
    own_stripes = pltpu.make_async_copy(outbox.at[st], inbox.at[st], load_sem.at[1])
    own_stripes.start()

    progress = [0, 1]

    def trickle():
        progress[0] += 1
        if progress[0] > TRS:
            stop = min(N_STORE, progress[1] + TRN)
            for d in range(progress[1], stop):
                fill((st + d) % N_STORE)
                stripe_copy(d).start()
            progress[1] = stop

    offsets = [0, -1, 1, -2, 2, -3, 3, 4]

    def send_across(i):
        send_w(slot(0, offsets[i]), slot(1, offsets[i]), ZFIRST, ys.at[i], yo.at[i], st_across)

    def ring(k):
        if k < 4:
            low, high = slot(0, -k), slot(0, k)
            arrived(w_at(low, FULL), zr.at[k])
            send_w(low, low, FULL if k < 3 else halves(FULL)[0], zs.at[2 * k], zr.at[k + 1], at_z(1))
            arrived(w_at(high, FULL), zl.at[k])
            send_w(high, high, FULL if k < 3 else halves(FULL)[1], zs.at[2 * k + 1], zl.at[k + 1], at_z(-1))
            send_across(2 * k - 1)
            send_across(2 * k)
        else:
            last = slot(0, 4)
            arrived(w_at(last, halves(FULL)[0]), zr.at[4])
            arrived(w_at(last, halves(FULL)[1]), zl.at[4])
            send_across(7)

    def line(k):
        if k == 0:
            chunk = slot(1, 0)
            arrived(w_at(chunk, FULL), yo.at[0])
            send_w(chunk, chunk, YFIRST, bs.at[0], br.at[1], at_z(1))
            send_w(chunk, chunk, YFIRST, bs.at[1], bl.at[1], at_z(-1))
        elif k < 4:
            low, high = slot(1, -k), slot(1, k)
            arrived(w_at(low, YFIRST), br.at[k])
            send_w(low, low, YFIRST if k < 3 else halves(YFIRST)[0], bs.at[2 * k], br.at[k + 1], at_z(1))
            arrived(w_at(high, YFIRST), bl.at[k])
            send_w(high, high, YFIRST if k < 3 else halves(YFIRST)[1], bs.at[2 * k + 1], bl.at[k + 1], at_z(-1))
        else:
            last = slot(1, 4)
            arrived(w_at(last, halves(YFIRST)[0]), br.at[4])
            arrived(w_at(last, halves(YFIRST)[1]), bl.at[4])

    def scale_pieces():
        for n in range(8):
            token, part, side = n // 2 % 2, n % 2, (near, far)[n // 4]
            arrived(half(piece_at(token, side, 1 - core), part), hs.at[n])
        for n in range(4):
            for copy in h_pass(n // 2, n % 2):
                copy.wait_send()
        for copy in h_sends:
            copy.wait_send()

        @pl.when(is_source)
        def _():
            for n in range(4):
                h_to_near(n // 2, n % 2).wait_send()

        @pl.when(jnp.logical_not(is_source))
        def _():
            for part in range(2):
                to_partner(part).wait_send()

        def block(b, carry):
            rows = pl.ds(pl.multiple_of(b * 32, 32), 32)
            for token in range(2):
                part = jnp.zeros((32, 1), jnp.float32)
                for p in range(4):
                    raw = hbuf[token * 4 + p, rows, :].astype(jnp.float32)
                    part += jnp.sum(raw * raw, axis=1, keepdims=True)
                    piece_gain = gains[p]
                    hbuf[token * 4 + p, rows, :] = (raw * piece_gain).astype(jnp.bfloat16)
                squares[token, rows, :] = jnp.broadcast_to(part, (32, HEAD))
            return carry

        gains = []
        for p in range(4):
            start = ((y if p < 2 else y_across) * 2 + p % 2) * FEATS
            columns = pl.ds(pl.multiple_of(start, FEATS), FEATS)
            gains.append(gain[columns].astype(jnp.float32).reshape(1, FEATS))
        lax.fori_loop(0, SLOTS // 32, block, 0)

    def project(m, side):
        token, part = m // 2, m % 2
        for c in range(2):
            weights = wbuf[side * NZ + c * 4 : side * NZ + c * 4 + 4].reshape(4 * CHUNK, COLS)
            product = jnp.dot(
                hbuf[token * 4 + side * 2 + c, part * 256 : part * 256 + 256, :],
                weights,
                preferred_element_type=jnp.float32,
            )
            rows = slice(m * 256, (m + 1) * 256)
            if side + c == 0:
                acc[rows, :] = product
            else:
                acc[rows, :] += product

    trickle()
    ring(1)
    trickle()
    other_step(0, 0)
    line(0)
    trickle()
    source_step(0)
    ring(2)
    trickle()
    line(1)
    trickle()
    other_step(0, 1)
    source_step(1)
    ring(3)
    trickle()
    line(2)
    trickle()
    h_far(0, 0)
    ring(4)
    trickle()
    other_step(1, 0)
    line(3)
    trickle()
    h_far(0, 1)
    other_step(1, 1)
    trickle()
    line(4)
    trickle()
    for d in range(progress[1], N_STORE):
        fill((st + d) % N_STORE)
        stripe_copy(d).start()

    lane = lax.broadcasted_iota(jnp.int32, (TILE, HEAD), 1)
    frequency = jnp.exp((lane % (HEAD // 2)).astype(jnp.float32) * (-math.log(500000.0) * 2.0 / HEAD))
    for s in range(SLOTS // TILE):
        position = lax.broadcasted_iota(jnp.int32, (TILE, HEAD), 0) + tiles[0, s] * TILE
        angle = position.astype(jnp.float32) * frequency
        turn[0, s] = jnp.cos(angle)
        turn[1, s] = jnp.where(lane < HEAD // 2, -jnp.sin(angle), jnp.sin(angle))

    h_far(1, 0)
    h_far(1, 1)
    scale_pieces()
    late = []
    send(squares.at[1], squares_in, ss.at[0], sr.at[0], st_partner, tp, late)

    for m in (2, 3):
        project(m, 0)
    for i in range(1, NZ):
        arrived(w_at(slot(1, offsets[i]), ZFIRST), yo.at[i])
    for part in range(2):
        rows = pl.ds(part * 256, 256)
        project(2 + part, 1)
        partial[rows, :] = acc[SLOTS + part * 256 : SLOTS + part * 256 + 256, :].astype(jnp.bfloat16)
        send(
            partial.at[rows, :], partial_in.at[rows, :], ss.at[1 + part], sr.at[1 + part], st_partner, tp, late
        )
    for m in (0, 1):
        project(m, 0)
        project(m, 1)
    arrived(squares_in, sr.at[0])
    for part in range(2):
        arrived(partial_in.at[pl.ds(part * 256, 256), :], sr.at[1 + part])

    for s in range(SLOTS // TILE):
        rows = slice(s * TILE, (s + 1) * TILE)
        scale = lax.rsqrt((squares[0, rows, :] + squares_in[rows, :]) / (N_TP * FEATS) + 1e-05)
        for h in range(6):
            columns = slice(h * HEAD, (h + 1) * HEAD)
            vec = (acc[rows, columns] + partial_in[rows, columns].astype(jnp.float32)) * scale
            turned = vec * turn[0, s] + pltpu.roll(vec, HEAD // 2, 1) * turn[1, s]
            if h < 4:
                q_out[h, rows, :] = turned.astype(jnp.bfloat16)
            elif h == 4:
                kv_out[rows, 0:HEAD] = turned.astype(jnp.bfloat16)
            else:
                kv_out[rows, HEAD : 2 * HEAD] = vec.astype(jnp.bfloat16)

    def stripe_wait(d, carry):
        other = (st - d + N_STORE) % N_STORE
        arrived(inbox.at[other], pr.at[d])
        stripe_copy(d).wait_send()
        id_copy(d).wait_send()
        return carry

    lax.fori_loop(1, N_STORE, stripe_wait, 0)
    own_stripes.wait()
    for copy in pending + late:
        copy.wait_send()


def exchange(hidden, gain, wq, km, vm, cache, ids, tiles):
    any_space = pl.BlockSpec(memory_space=pl.ANY)
    vmem = pl.BlockSpec(memory_space=pltpu.VMEM)
    smem = pl.BlockSpec(memory_space=pltpu.SMEM)
    dma = pltpu.SemaphoreType.DMA
    return pl.pallas_call(
        exchange_kernel,
        out_shape=[
            jax.ShapeDtypeStruct((4, SLOTS, HEAD), jnp.bfloat16),
            jax.ShapeDtypeStruct((SLOTS, 2 * HEAD), jnp.bfloat16),
            jax.ShapeDtypeStruct((N_STORE, PASSAGES * STRIPE, 2 * HEAD), jnp.bfloat16),
        ],
        in_specs=[any_space, vmem, any_space, any_space, any_space, any_space, vmem, smem],
        out_specs=[vmem, vmem, any_space],
        scratch_shapes=[
            pltpu.VMEM((SLOTS, FEATS), jnp.bfloat16),
            pltpu.VMEM((N_TP, SLOTS, FEATS), jnp.bfloat16),
            pltpu.VMEM((2 * NZ, CHUNK, COLS), jnp.bfloat16),
            pltpu.VMEM((128, STRIPE, 2 * HEAD), jnp.bfloat16),
            pltpu.VMEM((N_STORE, PASSAGES * STRIPE, 2 * HEAD), jnp.bfloat16),
            pltpu.VMEM((1, 128), jnp.int32),
            pltpu.VMEM((N_STORE, 1, 128), jnp.int32),
            pltpu.SMEM((N_STORE, 1, 128), jnp.int32),
            pltpu.VMEM((2 * SLOTS, COLS), jnp.float32),
            pltpu.VMEM((2, 4, TILE, HEAD), jnp.float32),
            pltpu.VMEM((2, SLOTS, HEAD), jnp.float32),
            pltpu.VMEM((SLOTS, HEAD), jnp.float32),
            pltpu.VMEM((SLOTS, COLS), jnp.bfloat16),
            pltpu.VMEM((SLOTS, COLS), jnp.bfloat16),
            dma((5,)),
            dma((5,)), dma((5,)), dma((8,)), dma((5,)), dma((5,)), dma((2,)), dma((4,)), dma((4,)), dma((8,)),
            dma((32,)), dma((32,)), dma((3,)),
            dma((8,)), dma((8,)), dma((8,)), dma((2,)), dma((4,)), dma((4,)), dma((8,)), dma((32,)), dma((32,)), dma((3,)),
        ],
        compiler_params=pltpu.CompilerParams(
            collective_id=0, has_side_effects=True, vmem_limit_bytes=62 * 2**20
        ),
    )(hidden, gain, wq, km, vm, cache, ids, tiles)


KEYS = 1024
STR = KEYS // STRIPE
PER = 1024 // KEYS


def attend_kernel(ids, placement, tiles, count, q, kv, inbox, out, stripes, scores, highest, total, values, sem):
    load = pltpu.make_async_copy(inbox, stripes, sem)
    load.start()
    load.wait()

    def block_of(b, lanes):
        j = b // PER
        first = b % PER * STR + N_STORE - placement[ids[0, j]]
        rows = pl.ds(pl.multiple_of(j * STRIPE, STRIPE), STRIPE)
        return jnp.concatenate([stripes[(first + k) % N_STORE, rows, lanes] for k in range(STR)], axis=0)

    for s in range(SLOTS // TILE):
        @pl.when(s < count[0])
        def _():
            j = tiles[0, s] // 8
            first = tiles[0, s] % 8 * 4 + N_STORE - placement[ids[0, j]]
            rows = pl.ds(pl.multiple_of(j * STRIPE, STRIPE), STRIPE)
            for k in range(4):
                part = s * TILE + k * STRIPE
                stripes[(first + k) % N_STORE, rows, :] = kv[part : part + STRIPE, :]

    def one_slot(s, carry):
        slot_rows = pl.ds(pl.multiple_of(s * TILE, TILE), TILE)

        @pl.when(s >= count[0])
        def _():
            out[slot_rows, :] = jnp.zeros((TILE, 4 * HEAD), jnp.bfloat16)

        @pl.when(s < count[0])
        def _():
            tile = tiles[0, s]
            last = tile // (KEYS // TILE)
            query = q[:, slot_rows, :].reshape(4 * TILE, HEAD)

            def block_scores(b):
                return lax.dot_general(
                    query, block_of(b, slice(0, HEAD)), (((1,), (1,)), ((), ())), preferred_element_type=jnp.float32
                )

            def widest(block):
                top = block[:, 0:HEAD]
                for n in range(1, KEYS // HEAD):
                    top = jnp.maximum(top, block[:, n * HEAD : (n + 1) * HEAD])
                return top

            block = block_scores(last)
            row = lax.broadcasted_iota(jnp.int32, (4 * TILE, KEYS), 0) % TILE + tile * TILE
            column = lax.broadcasted_iota(jnp.int32, (4 * TILE, KEYS), 1) + last * KEYS
            block = jnp.where(column <= row, block, -jnp.inf)
            scores[last] = block
            highest[...] = widest(block)

            def first_step(b):
                block = block_scores(b)
                scores[b] = block
                highest[...] = jnp.maximum(highest[...], widest(block))

            def second_step(b):
                terms = jnp.exp2(scores[b] * SCORE - shift)
                part = terms[:, 0:HEAD]
                for n in range(1, KEYS // HEAD):
                    part = part + terms[:, n * HEAD : (n + 1) * HEAD]
                total[...] += part
                values[...] += jnp.dot(
                    terms.astype(jnp.bfloat16), block_of(b, slice(HEAD, 2 * HEAD)), preferred_element_type=jnp.float32
                )

            def over(step, n):
                def pair(i, carry):
                    step(2 * i)
                    step(2 * i + 1)
                    return carry

                lax.fori_loop(0, n // 2, pair, 0)

                @pl.when(n % 2 == 1)
                def _():
                    step(n - 1)

            over(first_step, last)
            shift = jnp.max(highest[...], axis=1, keepdims=True) * SCORE
            total[...] = jnp.zeros_like(total)
            values[...] = jnp.zeros_like(values)
            over(second_step, last + 1)
            result = values[...] / jnp.sum(total[...], axis=1, keepdims=True)
            for h in range(4):
                out[slot_rows, h * HEAD : (h + 1) * HEAD] = result[h * TILE : (h + 1) * TILE, :].astype(jnp.bfloat16)

        return carry

    lax.fori_loop(0, SLOTS // TILE, one_slot, 0)

def attend(ids, placement, tiles, count, q, kv, inbox):
    vmem = pl.BlockSpec(memory_space=pltpu.VMEM)
    smem = pl.BlockSpec(memory_space=pltpu.SMEM)
    return pl.pallas_call(
        attend_kernel,
        out_shape=jax.ShapeDtypeStruct((SLOTS, 4 * HEAD), jnp.bfloat16),
        in_specs=[smem, smem, smem, smem, vmem, vmem, pl.BlockSpec(memory_space=pl.ANY)],
        out_specs=vmem,
        scratch_shapes=[
            pltpu.VMEM((N_STORE, PASSAGES * STRIPE, 2 * HEAD), jnp.bfloat16),
            pltpu.VMEM((PASSAGES * 1024 // KEYS, 4 * TILE, KEYS), jnp.float32),
            pltpu.VMEM((4 * TILE, HEAD), jnp.float32),
            pltpu.VMEM((4 * TILE, HEAD), jnp.float32),
            pltpu.VMEM((4 * TILE, HEAD), jnp.float32),
            pltpu.SemaphoreType.DMA,
        ],
        compiler_params=pltpu.CompilerParams(vmem_limit_bytes=62 * 2**20),
    )(ids, placement, tiles, count, q, kv, inbox)


def local(hidden, gain, w_query, key_matrix, value_matrix, passage_cache, passage_ids, placement, tile_index, tile_count):
    q, kv, inbox = exchange(
        hidden, gain, w_query, key_matrix, value_matrix, passage_cache, passage_ids, tile_index
    )
    return attend(passage_ids, placement, tile_index, tile_count, q, kv, inbox)


def solution(mesh):
    placed = (
        P("store", "tp"), P(), P("store", "tp"), P("store", "tp"), P("store", "tp"),
        P(None, "store", "tp"), P("store", None), P(), P("store", None), P("store"),
    )
    return jax.shard_map(local, mesh=mesh, in_specs=placed, out_specs=P("store", "tp"), check_vma=False)
```
